32 devices in a mesh: lat: 4 (over z), slab: 8 (over y, x, core).
Axes of the slice: x: 2, y: 2, z: 4, core: 2. Of those that a mesh axis runs over, the one named last changes fastest.
Arguments:
- field_state: float32 [4, 32, 32, 5, 128], P('lat', 'slab'), may hold values from -6 to 6
- cotangent: float32 [4, 32, 32, 5, 128], P('lat', None, 'slab'), may hold values from -6 to 6
- vertical_weight: float32 [4, 32, 32, 128], P('lat', 'slab'), may hold values from 0 to 1
- diffusion_inverse: float32 [4, 5, 32, 32], P('lat'), as said below
- source_row: int32 [4, 8, 4, 8, 8], P('lat', 'slab'), may hold values from 0 to 95, as said below
- dest_slot: int32 [4, 8, 128], P('lat', 'slab'), may hold values from 0 to 255, as said below
Outputs:
- tangent_out: float32 [4, 32, 32, 5, 128], P('lat', None, 'slab')
- adjoint_out: float32 [4, 32, 32, 5, 128], P('lat', 'slab')
The draws below stay inside these ranges and needn't reach their ends.
Inputs may be any that keep to these rules, and one draw needn't show every extreme that they name: `source_row`: from one sender to one receiver at most 8 slots are used, the used ones first; unused slots hold 0. Every value is below (3) * 32. `dest_slot`: each device's arrival rows name distinct used slots, and every used slot aimed at that device is named once; some sender fills all 8 slots to a receiver in every draw. `diffusion_inverse`: dense matrices of order one.
All inputs are finite; a program needn't handle non-finite values.
Results may differ from the reference program's by a relative error of at most 0.00007.
Values sent between devices are 32-bit elements; how exact they have to be, the bound alone decides.
No kernel may reach another device: no remote copies, remote signals or barrier semaphores. Data moves between devices by JAX's collectives and lax.ppermute only.
A program may use at most 128 MiB of HBM per device.

```python
import math
import jax
import jax.numpy as jnp
from jax import lax

F = 5
BW = 128
LEV_DEV = 4
BLOCKS = 32
LEV = 32
CAP = 8
N_LAT = 4
N_SLAB = 8


def routes(key):
    key = jax.random.fold_in(key, 7)
    key_base, key_perm, key_rows = jax.random.split(key, 3)
    devices_all = N_LAT * N_SLAB
    row_total = LEV_DEV * BLOCKS
    slot_total = devices_all * CAP
    ranks = jnp.arange(devices_all, dtype=jnp.int32)
    group_gap = jnp.abs(ranks[:, None] // N_SLAB - ranks[None, :] // N_SLAB)
    nearness = jnp.where(group_gap == 0, 2000, jnp.where(group_gap == 1, 1000, 0))
    itself = jnp.where(ranks[:, None] == ranks[None, :], 100000, 0)
    base = jax.random.randint(key_base, (devices_all, devices_all), 0, 1000) + nearness + itself
    slot_ids = jnp.arange(CAP, dtype=jnp.int32)
    scores = base[:, :, None] - 300 * slot_ids[None, None, :]
    flat_ids = ranks[:, None] * CAP + slot_ids[None, :]
    keyed = (scores * slot_total + flat_ids[None, :, :]).reshape(devices_all, slot_total)
    unused_vals, chosen = lax.top_k(keyed, row_total)
    chosen = chosen.astype(jnp.int32)

    def shuffle(key_row, row_ids):
        return jax.random.permutation(key_row, row_ids)
    dest_all = jax.vmap(shuffle)(jax.random.split(key_perm, devices_all), chosen)
    used = jnp.zeros((devices_all, slot_total), jnp.int32).at[ranks[:, None], chosen].set(1)
    picks = jax.random.randint(key_rows, (devices_all, slot_total), 0, (LEV_DEV - 1) * BLOCKS) * used
    source_all = picks.reshape(devices_all, devices_all, CAP).transpose(1, 0, 2)
    return (source_all.reshape(N_LAT, N_SLAB, N_LAT, N_SLAB, CAP), dest_all.reshape(N_LAT, N_SLAB, row_total))


def draw_source_row(key, part):
    return routes(key)[0]


def draw_dest_slot(key, part):
    return routes(key)[1]


def draw_diffusion_inverse(key, part):
    rows_ids = jnp.arange(LEV, dtype=jnp.int32)
    identity = jnp.where(rows_ids[:, None] == rows_ids[None, :], 1.0, 0.0).astype(jnp.float32)
    noise = jax.random.normal(key, (N_LAT, F, LEV, LEV), jnp.float32)
    return 0.9 * identity + noise * (0.5 / math.sqrt(LEV))


def block_levels(stream_key, dims, cuts, smallest, largest):
    loudness = 1.0
    for axis_at, parts in cuts:
        heights = jax.random.uniform(jax.random.fold_in(jax.random.fold_in(stream_key, 6), axis_at), (parts,), jnp.float32, smallest / len(cuts), largest / len(cuts))
        loudness = loudness * jnp.repeat(jnp.exp(heights), dims[axis_at] // parts).reshape((-1,) + (1,) * (len(dims) - 1 - axis_at))
    return loudness


def centred(key, shape, spread, most, pieces=(), kind=jnp.bfloat16):
    entries = spread * jax.random.normal(key, shape, jnp.float32)
    if pieces:
        entries = entries * block_levels(key, shape, pieces, -0.22, 0.18)
    return jnp.clip(entries, -most, most).astype(kind)


def setup_inputs(seed: int = 0) -> dict:
    key_list = jax.random.split(jax.random.key(seed), 7)
    field_state = centred(key_list[0], (N_LAT, LEV, BLOCKS, F, BW), 1.0, 6.0, ((0, 4), (1, 8)), jnp.float32)
    cotangent = centred(key_list[1], (N_LAT, LEV, BLOCKS, F, BW), 1.0, 6.0, ((0, 4), (2, 8)), jnp.float32)
    vertical_weight = jnp.clip(1.0 * jax.random.uniform(key_list[2], (N_LAT, LEV, BLOCKS, BW), jnp.float32) ** block_levels(key_list[2], (N_LAT, LEV, BLOCKS, BW), ((0, 4), (1, 8)), -0.2, 0.2), 0.0, 1.0)
    diffusion_inverse = draw_diffusion_inverse(jax.random.fold_in(key_list[6], 71), 0)
    source_row = draw_source_row(jax.random.fold_in(key_list[6], 71), 0)
    dest_slot = draw_dest_slot(jax.random.fold_in(key_list[6], 71), 0)
    return dict(field_state=field_state, cotangent=cotangent, vertical_weight=vertical_weight, diffusion_inverse=diffusion_inverse, source_row=source_row, dest_slot=dest_slot)


def reference(field_state, cotangent, vertical_weight, diffusion_inverse, source_row, dest_slot):
    highest = lax.Precision.HIGHEST
    devices_all = N_LAT * N_SLAB
    row_total = LEV_DEV * BLOCKS
    level_rows = field_state.reshape(devices_all * row_total, F, BW)
    weights = vertical_weight.reshape(devices_all, row_total, 1, BW)
    sender_first = source_row.reshape(devices_all, devices_all, CAP)
    slots = dest_slot.reshape(devices_all, row_total)
    sender = slots // CAP
    within = slots % CAP
    receiver = jnp.arange(devices_all, dtype=jnp.int32)[:, None]
    lower_idx = (sender * row_total + sender_first[sender, receiver, within]).astype(jnp.int32)
    upper_idx = (lower_idx + BLOCKS).astype(jnp.int32)
    lower_vals = level_rows[lower_idx]
    upper_vals = level_rows[upper_idx]
    moved = (1.0 - weights) * lower_vals + weights * upper_vals
    moved = moved.reshape(N_LAT, LEV, BLOCKS, F, BW)
    tangent_out = jnp.einsum('gflk,gkbfc->glbfc', diffusion_inverse, moved, precision=highest)
    back = jnp.einsum('gflk,glbfc->gkbfc', diffusion_inverse, cotangent, precision=highest)
    back = back.reshape(devices_all, row_total, F, BW)
    adjoint = jnp.zeros((devices_all * row_total, F, BW), jnp.float32)
    adjoint = adjoint.at[lower_idx.reshape(-1)].add(((1.0 - weights) * back).reshape(-1, F, BW))
    adjoint = adjoint.at[upper_idx.reshape(-1)].add((weights * back).reshape(-1, F, BW))
    return tangent_out, adjoint.reshape(N_LAT, LEV, BLOCKS, F, BW)
```

```python
import functools

import jax
import jax.numpy as jnp
from jax import lax
from jax.experimental import pallas as pl
from jax.experimental.pallas import tpu as pltpu
from jax.sharding import PartitionSpec as P

LANES = 128
HIGHEST = lax.Precision.HIGHEST


def parts_of(values):
    high = values.astype(jnp.bfloat16)
    rest = values - high.astype(jnp.float32)
    mid = rest.astype(jnp.bfloat16)
    low = (rest - mid.astype(jnp.float32)).astype(jnp.bfloat16)
    return low, mid, high


def pick(table, values, contract):
    total = None
    for part in parts_of(values):
        term = lax.dot_general(
            table, part, ((contract, (0,)), ((), ())), preferred_element_type=jnp.float32
        )
        total = term if total is None else total + term
    return total


def hot(rows, wanted):
    return jnp.where(rows == wanted, 1.0, 0.0).astype(jnp.bfloat16)


def sizes(mesh_lat, mesh_slab, cap):
    return mesh_lat, mesh_slab, mesh_slab // 2, cap


def start_kernel(dims, me, cot, inverse, weights, dest, *rest):
    lats, slabs, chips, cap, lev_dev, here, fields = dims
    out_back, out_w = rest[:chips], rest[chips : 2 * chips]
    back, = rest[2 * chips :]
    chip = me[1]
    levels = slabs * lev_dev
    step = fields * here
    span = lev_dev * here
    for f in range(fields):
        wide = jnp.concatenate(
            [cot[pl.ds(f * here + b, levels, stride=step), :] for b in range(here)], axis=1
        )
        res = lax.dot_general(
            inverse[f], wide, (((0,), (0,)), ((), ())), precision=HIGHEST, preferred_element_type=jnp.float32
        )
        for b in range(here):
            back[f, pl.ds(b, levels, stride=here), :] = res[:, b * LANES : (b + 1) * LANES]
    for k in range(chips):
        other = jnp.bitwise_xor(chip, k)
        for h in range(2):
            first = pl.multiple_of((other * 2 + h) * span, span)
            for f in range(fields):
                out_back[k][h, f] = back[f, pl.ds(first, span), :]
    slots = slabs * cap
    rows = lax.broadcasted_iota(jnp.int32, (slots, dest.shape[1]), 0)
    for k in range(chips):
        other = jnp.bitwise_xor(chip, k)
        per = lats * cap
        local = lax.broadcasted_iota(jnp.int32, (2 * per, dest.shape[1]), 0)
        half = local // per
        lat = (local - half * per) // cap
        slot = local - half * per - lat * cap
        wanted = lat * slots + (other * 2 + half) * cap + slot
        res = pick(hot(wanted, dest[...]), weights[...], (1,))
        for h in range(2):
            for g in range(lats):
                at = (h * lats + g) * cap
                out_w[k][h, g] = res[at : at + cap]


def back_kernel(dims, me, dest, *rest):
    lats, slabs, chips, cap, lev_dev, here, fields = dims
    got, out, rows = rest[: 2 * chips], rest[2 * chips : 3 * chips], rest[3 * chips]
    chip, core = me[1], me[2]
    span = lev_dev * here
    for k in range(chips):
        for x in range(2):
            src = jnp.bitwise_xor(chip, k) * 2 + jnp.bitwise_xor(core, x)
            first = pl.multiple_of(src * span, span)
            for f in range(fields):
                rows[pl.ds(first, span), f * LANES : (f + 1) * LANES] = got[2 * k + x][core, f]
    values = rows[...]
    slots = slabs * cap
    per = lats * cap
    local = lax.broadcasted_iota(jnp.int32, (2 * per, dest.shape[1]), 0)
    half = local // per
    lat = (local - half * per) // cap
    slot = local - half * per - lat * cap
    tables = []
    for k in range(chips):
        wanted = lat * slots + (jnp.bitwise_xor(chip, k) * 2 + half) * cap + slot
        tables.append(hot(wanted, dest[...]))
    res = pick(jnp.concatenate(tables, axis=0), values, (1,))
    for k in range(chips):
        for h in range(2):
            for g in range(lats):
                at = ((k * 2 + h) * lats + g) * cap
                for f in range(fields):
                    out[k][h, g, f] = res[at : at + cap, f * LANES : (f + 1) * LANES]


def gather_kernel(dims, me, *rest):
    lats, slabs, chips, cap, lev_dev, here, fields = dims
    got, got_w, out = rest[: 2 * chips], rest[2 * chips : 4 * chips], rest[4 * chips :]
    lat, chip, core = me[0], me[1], me[2]
    for j in range(lats):
        other = jnp.bitwise_xor(lat, j)
        for k in range(chips):
            for x in range(2):
                src = jnp.bitwise_xor(chip, k) * 2 + jnp.bitwise_xor(core, x)
                for f in range(fields):
                    out[j][f, src] = got[2 * k + x][core, other, f]
                out[j][fields, src] = got_w[2 * k + x][core, other]


def add_kernel(dims, me, source, *rest):
    lats, slabs, chips, cap, lev_dev, here, fields = dims
    got, out = rest[:lats], rest[lats]
    blocks = slabs * here
    row_total = lev_dev * blocks
    slots = slabs * cap
    lat = me[0]
    row = lax.broadcasted_iota(jnp.int32, (row_total, slots), 0)
    total = None
    for j in range(lats):
        low = source[jnp.bitwise_xor(lat, j)]
        weight = got[j][fields].reshape(slots, LANES)
        scale = jnp.concatenate([weight] * fields, axis=1)
        values = jnp.concatenate([got[j][f].reshape(slots, LANES) for f in range(fields)], axis=1)
        both = jnp.concatenate([(1.0 - scale) * values, scale * values], axis=0)
        table = jnp.concatenate([hot(row, low), hot(row, low + blocks)], axis=1)
        term = pick(table, both, (1,))
        total = term if total is None else total + term
    for l in range(lev_dev):
        for f in range(fields):
            out[l, f] = total[l * blocks : (l + 1) * blocks, f * LANES : (f + 1) * LANES]


def mix_kernel(dims, me, *rest):
    lats, slabs, chips, cap, lev_dev, here, fields = dims
    state, source, got_w = rest[:lats], rest[lats : 2 * lats], rest[2 * lats : 2 * lats + 2 * chips]
    out = rest[2 * lats + 2 * chips : 2 * lats + 3 * chips]
    weight, mixed = rest[2 * lats + 3 * chips :]
    lat, chip, core = me[0], me[1], me[2]
    blocks = slabs * here
    row_total = lev_dev * blocks
    slots = slabs * cap
    for k in range(chips):
        for x in range(2):
            src = jnp.bitwise_xor(chip, k) * 2 + jnp.bitwise_xor(core, x)
            for g in range(lats):
                weight[g, src] = got_w[2 * k + x][core, g]
    row = lax.broadcasted_iota(jnp.int32, (row_total, slots), 0)
    for j in range(lats):
        sender = jnp.bitwise_xor(lat, j)
        low = source[j][lat]
        values = jnp.concatenate(
            [state[j][:, f].reshape(row_total, LANES) for f in range(fields)], axis=1
        )
        table = jnp.concatenate([hot(row, low), hot(row, low + blocks)], axis=1)
        both = pick(table, values, (0,))
        scale = jnp.concatenate([weight[sender].reshape(slots, LANES)] * fields, axis=1)
        res = (1.0 - scale) * both[:slots] + scale * both[slots:]
        for s in range(slabs):
            for f in range(fields):
                mixed[s, f] = res[s * cap : (s + 1) * cap, f * LANES : (f + 1) * LANES]
        for k in range(chips):
            for h in range(2):
                to = jnp.bitwise_xor(chip, k) * 2 + h
                out[k][h, sender] = mixed[to]


def arrive_kernel(dims, me, dest, *rest):
    lats, slabs, chips, cap, lev_dev, here, fields = dims
    got, out = rest[: 2 * chips], rest[2 * chips : 3 * chips]
    rows, moved = rest[3 * chips :]
    chip, core = me[1], me[2]
    span = lev_dev * here
    slots = slabs * cap
    for k in range(chips):
        for x in range(2):
            src = jnp.bitwise_xor(chip, k) * 2 + jnp.bitwise_xor(core, x)
            for g in range(lats):
                for f in range(fields):
                    rows[f, g * slabs + src] = got[2 * k + x][core, g, f]
    values = jnp.concatenate([rows[f].reshape(lats * slots, LANES) for f in range(fields)], axis=1)
    slot = lax.broadcasted_iota(jnp.int32, (lats * slots, dest.shape[1]), 0)
    res = pick(hot(slot, dest[...]), values, (0,))
    for s in range(slabs):
        for f in range(fields):
            moved[s, f] = res[s * span : (s + 1) * span, f * LANES : (f + 1) * LANES]
    for k in range(chips):
        for h in range(2):
            out[k][h] = moved[jnp.bitwise_xor(chip, k) * 2 + h]


def diffuse_kernel(dims, me, inverse, *rest):
    lats, slabs, chips, cap, lev_dev, here, fields = dims
    got, out, rows = rest[: 2 * chips], rest[2 * chips], rest[2 * chips + 1]
    chip, core = me[1], me[2]
    span = lev_dev * here
    levels = slabs * lev_dev
    for k in range(chips):
        for x in range(2):
            src = jnp.bitwise_xor(chip, k) * 2 + jnp.bitwise_xor(core, x)
            first = pl.multiple_of(src * span, span)
            for f in range(fields):
                rows[f, pl.ds(first, span), :] = got[2 * k + x][core, f]
    for f in range(fields):
        wide = jnp.concatenate(
            [rows[f, pl.ds(b, levels, stride=here), :] for b in range(here)], axis=1
        )
        res = jnp.dot(inverse[f], wide, precision=HIGHEST, preferred_element_type=jnp.float32)
        for b in range(here):
            out[pl.ds(f * here + b, levels, stride=fields * here), :] = res[:, b * LANES : (b + 1) * LANES]


def call(kernel, dims, args, outs, scratch=()):
    f32 = jnp.float32
    specs = [pl.BlockSpec(memory_space=pltpu.SMEM)] + [pl.BlockSpec(memory_space=pltpu.VMEM)] * (len(args) - 1)
    return pl.pallas_call(
        functools.partial(kernel, dims),
        out_shape=[jax.ShapeDtypeStruct(shape, f32) for shape in outs],
        in_specs=specs,
        out_specs=[pl.BlockSpec(memory_space=pltpu.VMEM)] * len(outs),
        scratch_shapes=[pltpu.VMEM(shape, f32) for shape in scratch],
        compiler_params=pltpu.CompilerParams(vmem_limit_bytes=48 * 1024 * 1024),
    )(*args)


def swap(array, axis, bit, count):
    return lax.ppermute(array, axis, [(i, i ^ bit) for i in range(count)])


def over_slab(messages, slabs):
    got = []
    for k, message in enumerate(messages):
        arrived = message if k == 0 else swap(message, "slab", 2 * k, slabs)
        got += [arrived, swap(arrived, "slab", 1, slabs)]
    return got


def body(lats, slabs, field_state, cotangent, vertical_weight, diffusion_inverse, source_row, dest_slot):
    _, lev_dev, blocks, fields, width = field_state.shape
    cap = source_row.shape[-1]
    chips = slabs // 2
    here = blocks // slabs
    levels = slabs * lev_dev
    row_total = lev_dev * blocks
    span = lev_dev * here
    dims = (lats, slabs, chips, cap, lev_dev, here, fields)
    lat, slab = lax.axis_index("lat"), lax.axis_index("slab")
    me = jnp.stack([lat, slab // 2, slab % 2]).astype(jnp.int32)

    state = field_state[0].transpose(0, 2, 1, 3)
    cot = cotangent[0].transpose(0, 2, 1, 3).reshape(levels * fields * here, width)
    weights = vertical_weight.reshape(row_total, width)
    inverse = diffusion_inverse[0]
    dest = dest_slot[0]
    dest_sorted = dest.reshape(lev_dev, slabs, here).transpose(1, 0, 2).reshape(1, row_total)
    source = source_row.reshape(lats, 1, slabs * cap)

    states, sources = [state], [source]
    for j in range(1, lats):
        if j % 2 == 0 or j == 1:
            states.append(swap(state, "lat", j, lats))
        else:
            states.append(swap(states[j - 1], "lat", 1, lats))
        sources.append(swap(source, "lat", j, lats))

    first = call(
        start_kernel,
        dims,
        (me, cot, inverse, weights, dest),
        [(2, fields, span, width)] * chips + [(2, lats, cap, width)] * chips,
        [(fields, levels * here, width)],
    )
    back = over_slab(first[:chips], slabs)
    slot_weight = over_slab(first[chips:], slabs)

    slot_back = call(
        back_kernel,
        dims,
        (me, dest_sorted, *back),
        [(2, lats, fields, cap, width)] * chips,
        [(row_total, fields * width)],
    )
    sorted_back = call(
        gather_kernel,
        dims,
        (me, *over_slab(slot_back, slabs), *slot_weight),
        [(fields + 1, slabs, cap, width)] * lats,
    )
    returned = [message if j == 0 else swap(message, "lat", j, lats) for j, message in enumerate(sorted_back)]
    (adjoint,) = call(add_kernel, dims, (me, source, *returned), [(lev_dev, fields, blocks, width)])

    mixed = call(
        mix_kernel,
        dims,
        (me, *states, *sources, *slot_weight),
        [(2, lats, fields, cap, width)] * chips,
        [(lats, slabs, cap, width), (slabs, fields, cap, width)],
    )
    moved = call(
        arrive_kernel,
        dims,
        (me, dest_sorted, *over_slab(mixed, slabs)),
        [(2, fields, span, width)] * chips,
        [(fields, lats * slabs, cap, width), (slabs, fields, span, width)],
    )
    (tangent,) = call(
        diffuse_kernel,
        dims,
        (me, inverse, *over_slab(moved, slabs)),
        [(levels * fields * here, width)],
        [(fields, levels * here, width)],
    )
    tangent_out = tangent.reshape(1, levels, fields, here, width).transpose(0, 1, 3, 2, 4)
    adjoint_out = adjoint.transpose(0, 2, 1, 3)[None]
    return tangent_out, adjoint_out


def solution(mesh):
    placed = (
        P("lat", "slab", None, None, None),
        P("lat", None, "slab", None, None),
        P("lat", "slab", None, None),
        P("lat", None, None, None),
        P("lat", "slab", None, None, None),
        P("lat", "slab", None),
    )
    return jax.shard_map(
        functools.partial(body, mesh.shape["lat"], mesh.shape["slab"]),
        mesh=mesh,
        in_specs=placed,
        out_specs=(P("lat", None, "slab", None, None), P("lat", "slab", None, None, None)),
        check_vma=False,
    )
```

```python
import functools

import jax
import jax.numpy as jnp
from jax import lax
from jax.experimental import pallas as pl
from jax.experimental.pallas import tpu as pltpu
from jax.sharding import PartitionSpec as P

LANES = 128
F32 = jnp.float32
EXACT = functools.partial(lax.dot_general, precision=lax.Precision.HIGHEST, preferred_element_type=F32)
SHORT = functools.partial(lax.dot_general, preferred_element_type=F32)


def two_parts(values):
    high = values.astype(jnp.bfloat16)
    return high, (values - high.astype(F32)).astype(jnp.bfloat16)


def pick(table, values, contract):
    dims = ((contract, (0,)), ((), ()))
    high, low = two_parts(values)
    return SHORT(table, low, dims) + SHORT(table, high, dims)


def product(left, right, contract):
    dims = ((contract, (0,)), ((), ()))
    left_high, left_low = two_parts(left)
    right_high, right_low = two_parts(right)
    return (
        SHORT(left_low, right_high, dims)
        + SHORT(left_high, right_low, dims)
        + SHORT(left_high, right_high, dims)
    )


def hot(rows, wanted):
    return jnp.where(rows == wanted, 1.0, 0.0).astype(jnp.bfloat16)


def iota(shape, axis):
    return lax.broadcasted_iota(jnp.int32, shape, axis)


def xor(a, b):
    return jnp.bitwise_xor(a, b)


def pack_kernel(dims, me, state, source, out):
    lats, slabs, chips, cap, lev_dev, here, fields = dims
    total = state.shape[0]
    out[:total, :] = state[...]
    slots = slabs * cap
    spread = jnp.where(iota((cap, slots), 1) % cap == iota((cap, slots), 0), 1.0, 0.0)
    wide = EXACT(source[...].reshape(lats * slabs, cap).astype(F32), spread, (((1,), (0,)), ((), ())))
    mine = iota((slabs, slots), 1) // cap == iota((slabs, slots), 0)
    out[total:, :] = jnp.zeros((out.shape[0] - total, LANES), F32)
    for g in range(lats):
        row = jnp.where(mine, wide[g * slabs : (g + 1) * slabs], 0.0)
        out[total + g : total + g + 1, :slots] = jnp.sum(row, axis=0, keepdims=True)


def start_kernel(dims, me, cot, inverse, cot_pair, *rest):
    lats, slabs, chips, cap, lev_dev, here, fields = dims
    out, back = rest[:chips], rest[-1]
    chip, core = me[1], me[2]
    levels = slabs * lev_dev
    step = fields * here
    span = 2 * lev_dev * 2 * here
    for f in range(fields):
        own = [cot[pl.ds(f * here + b, levels, stride=step), :] for b in range(here)]
        pair = [cot_pair[pl.ds(f * here + b, levels, stride=step), :] for b in range(here)]
        own, pair = jnp.concatenate(own, axis=1), jnp.concatenate(pair, axis=1)
        wide = jnp.concatenate(
            [jnp.where(core == 0, own, pair), jnp.where(core == 0, pair, own)], axis=1
        )
        res = product(inverse[f], wide, (0,))
        for b in range(2 * here):
            back[f, pl.ds(b, levels, stride=2 * here), :] = res[:, b * LANES : (b + 1) * LANES]
    for k in range(chips):
        first = pl.multiple_of(xor(chip, k) * span, span)
        for f in range(fields):
            out[k][f] = back[f, pl.ds(first, span), :].reshape(2, span // 2, LANES)


def by_column_owner(dest, lev_dev, chips, wide):
    total = dest.shape[1]
    at = iota((total, total), 1)
    span = lev_dev * wide
    chip = at // span
    level = (at - chip * span) // wide
    block = at - chip * span - level * wide
    order = jnp.where(iota((total, total), 0) == (level * chips + chip) * wide + block, 1.0, 0.0)
    return EXACT(dest.astype(F32), order, (((1,), (0,)), ((), ()))).astype(jnp.int32)


def slot_table(dims, core, dest, by_chip):
    lats, slabs, chips, cap, lev_dev, here, fields = dims
    shape = (chips * lats * cap, dest.shape[1])
    at = iota(shape, 0)
    if by_chip:
        chip = at // (lats * cap)
        lat = at // cap - chip * lats
    else:
        lat = at // (chips * cap)
        chip = at // cap - lat * chips
    slot = at - at // cap * cap
    return hot(lat * (slabs * cap) + (chip * 2 + core) * cap + slot, dest)


def back_kernel(dims, me, dest, dest_pair, weight, weight_pair, *rest):
    lats, slabs, chips, cap, lev_dev, here, fields = dims
    got, out, dest_out = rest[:chips], rest[-chips - 3 : -3], rest[-3]
    rows, slots = rest[-2:]
    chip, core = me[1], me[2]
    wide = 2 * here
    span = lev_dev * wide
    both = by_column_owner(jnp.concatenate([dest[...], dest_pair[...]], axis=0), lev_dev, chips, wide)
    dest_out[...] = both
    for x, w in enumerate((weight, weight_pair)):
        r = xor(core, x)
        for k in range(chips):
            first = pl.multiple_of(xor(chip, k) * span, span)
            for f in range(fields):
                rows[x, pl.ds(first, span), f * LANES : (f + 1) * LANES] = got[k][f, r]
        for c in range(chips):
            for l in range(lev_dev):
                at = l * chips * wide + c * wide
                rows[x, c * span + l * wide : c * span + (l + 1) * wide, fields * LANES :] = w[at : at + wide]
        res = pick(slot_table(dims, core, both[x : x + 1], True), rows[x], (1,))
        for c in range(chips):
            for g in range(lats):
                at = (c * lats + g) * cap
                for f in range(fields + 1):
                    slots[c, g, f] = res[at : at + cap, f * LANES : (f + 1) * LANES]
        for k in range(chips):
            out[k][x] = slots[xor(chip, k)]


def sort_kernel(groups, dims, me, *rest):
    lats, slabs, chips, cap, lev_dev, here, fields = dims
    got, outs = rest[:chips], rest[-len(groups) :]
    lat, chip, core = me[0], me[1], me[2]
    for out, j in zip(outs, groups):
        other = xor(lat, j)
        for k in range(chips):
            for x in range(2):
                src = xor(chip, k) * 2 + xor(core, x)
                for f in range(fields + 1):
                    out[f, src] = got[k][x, other, f]


def add_kernel(dims, me, packed, *rest):
    lats, slabs, chips, cap, lev_dev, here, fields = dims
    got, out = rest[:lats], rest[-1]
    blocks = slabs * here
    row_total = lev_dev * blocks
    slots = slabs * cap
    lat = me[0]
    row = iota((row_total, slots), 0)
    tables, values = [], []
    for j in range(lats):
        at = fields * row_total + xor(lat, j)
        low = packed[pl.ds(at, 1), :][:, :slots].astype(jnp.int32)
        scale = jnp.concatenate([got[j][fields].reshape(slots, LANES)] * fields, axis=1)
        value = jnp.concatenate([got[j][f].reshape(slots, LANES) for f in range(fields)], axis=1)
        values += [(1.0 - scale) * value, scale * value]
        tables += [hot(row, low), hot(row, low + blocks)]
    total = pick(jnp.concatenate(tables, axis=1), jnp.concatenate(values, axis=0), (1,))
    for l in range(lev_dev):
        for f in range(fields):
            out[l, f] = total[l * blocks : (l + 1) * blocks, f * LANES : (f + 1) * LANES]


def hold_kernel(dims, me, array, *rest):
    out, sem = rest[-2:]
    copy = pltpu.make_async_copy(array, out, sem)
    copy.start()
    copy.wait()


def mix_kernel(dims, me, *rest):
    lats, slabs, chips, cap, lev_dev, here, fields = dims
    got, packed = rest[:chips], rest[chips : chips + lats]
    out, weight, mixed = rest[-chips - 2 : -2], rest[-2], rest[-1]
    lat, chip, core = me[0], me[1], me[2]
    blocks = slabs * here
    row_total = lev_dev * blocks
    slots = slabs * cap
    for k in range(chips):
        for x in range(2):
            src = xor(chip, k) * 2 + xor(core, x)
            for g in range(lats):
                weight[g, src] = got[k][x, g, fields]
    row = iota((row_total, slots), 0)
    for j in range(lats):
        sender = xor(lat, j)
        low = packed[j][pl.ds(fields * row_total + lat, 1), :][:, :slots].astype(jnp.int32)
        values = jnp.concatenate(
            [
                jnp.concatenate(
                    [packed[j][(l * fields + f) * blocks : (l * fields + f + 1) * blocks] for l in range(lev_dev)],
                    axis=0,
                )
                for f in range(fields)
            ],
            axis=1,
        )
        table = jnp.concatenate([hot(row, low), hot(row, low + blocks)], axis=1)
        both = pick(table, values, (0,))
        scale = jnp.concatenate([weight[sender].reshape(slots, LANES)] * fields, axis=1)
        res = (1.0 - scale) * both[:slots] + scale * both[slots:]
        for s in range(slabs):
            for f in range(fields):
                mixed[s, f] = res[s * cap : (s + 1) * cap, f * LANES : (f + 1) * LANES]
        for k in range(chips):
            for x in range(2):
                out[k][x, sender] = mixed[xor(chip, k) * 2 + xor(core, x)]


def arrive_kernel(dims, me, dest, *rest):
    lats, slabs, chips, cap, lev_dev, here, fields = dims
    got, out = rest[:chips], rest[-chips - 2 : -2]
    rows, moved = rest[-2:]
    chip, core = me[1], me[2]
    span = lev_dev * 2 * here
    for x in range(2):
        for k in range(chips):
            for g in range(lats):
                for f in range(fields):
                    rows[f, g * chips + xor(chip, k)] = got[k][x, g, f]
        values = jnp.concatenate(
            [rows[f].reshape(lats * chips * cap, LANES) for f in range(fields)], axis=1
        )
        res = pick(slot_table(dims, core, dest[x : x + 1, :], False), values, (0,))
        for c in range(chips):
            for f in range(fields):
                moved[c, f] = res[c * span : (c + 1) * span, f * LANES : (f + 1) * LANES]
        for k in range(chips):
            for f in range(fields):
                out[k][f, xor(core, x)] = moved[xor(chip, k), f]


def diffuse_kernel(dims, me, inverse, *rest):
    lats, slabs, chips, cap, lev_dev, here, fields = dims
    got, own, pair, rows = rest[:chips], rest[-3], rest[-2], rest[-1]
    chip, core = me[1], me[2]
    wide = 2 * here
    span = 2 * lev_dev * wide
    levels = slabs * lev_dev
    for k in range(chips):
        first = pl.multiple_of(xor(chip, k) * span, span)
        for f in range(fields):
            rows[f, pl.ds(first, span), :] = got[k][f].reshape(span, LANES)
    for f in range(fields):
        values = jnp.concatenate([rows[f, pl.ds(b, levels, stride=wide), :] for b in range(wide)], axis=1)
        res = product(inverse[f], values, (1,))
        first, second = res[:, : here * LANES], res[:, here * LANES :]
        mine, other = jnp.where(core == 0, first, second), jnp.where(core == 0, second, first)
        for b in range(here):
            at = pl.ds(f * here + b, levels, stride=fields * here)
            own[at, :] = mine[:, b * LANES : (b + 1) * LANES]
            pair[at, :] = other[:, b * LANES : (b + 1) * LANES]


def call(kernel, dims, args, outs, scratch=(), after=(), outside=()):
    inside = pl.BlockSpec(memory_space=pltpu.VMEM)
    anywhere = pl.BlockSpec(memory_space=pl.ANY)
    specs = [pl.BlockSpec(memory_space=pltpu.SMEM)]
    specs += [anywhere if i in outside else inside for i in range(1, len(args))]
    return pl.pallas_call(
        functools.partial(kernel, dims),
        out_shape=[shape if hasattr(shape, "dtype") else jax.ShapeDtypeStruct(shape, F32) for shape in outs],
        in_specs=specs + [anywhere] * len(after),
        out_specs=[inside] * len(outs),
        scratch_shapes=[pltpu.VMEM(shape, F32) if isinstance(shape, tuple) else shape for shape in scratch],
        compiler_params=pltpu.CompilerParams(vmem_limit_bytes=48 * 1024 * 1024),
    )(*args, *after)


def swap(array, axis, bit, count):
    return lax.ppermute(array, axis, [(i, i ^ bit) for i in range(count)])


def body(lats, slabs, field_state, cotangent, vertical_weight, diffusion_inverse, source_row, dest_slot):
    _, lev_dev, blocks, fields, width = field_state.shape
    cap = source_row.shape[-1]
    chips = slabs // 2
    here = blocks // slabs
    levels = slabs * lev_dev
    row_total = lev_dev * blocks
    span = lev_dev * 2 * here
    dims = (lats, slabs, chips, cap, lev_dev, here, fields)
    lat, slab = lax.axis_index("lat"), lax.axis_index("slab")
    me = jnp.stack([lat, slab // 2, slab % 2]).astype(jnp.int32)

    def pair(array):
        return swap(array, "slab", 1, slabs)

    def over_chips(messages):
        return [m if k == 0 else swap(m, "slab", 2 * k, slabs) for k, m in enumerate(messages)]

    state = field_state[0].transpose(0, 2, 1, 3).reshape(row_total * fields, width)
    cot = cotangent[0].transpose(0, 2, 1, 3).reshape(levels * fields * here, width)
    weights = vertical_weight.reshape(row_total, width)
    inverse = diffusion_inverse[0]
    dest = dest_slot[0]

    (packed,) = call(
        pack_kernel,
        dims,
        (me, state, source_row[0, 0]),
        [(row_total * fields + -(-lats // 8) * 8, width)],
    )
    near, far = swap(packed, "lat", 1, lats), swap(packed, "lat", 2, lats)
    first = call(
        start_kernel,
        dims,
        (me, cot, inverse, pair(cot)),
        [(fields, 2, span, width)] * chips,
        [(fields, levels * 2 * here, width)],
    )
    *slot_back, dests = call(
        back_kernel,
        dims,
        (me, dest, pair(dest), weights, pair(weights), *over_chips(first)),
        [(2, lats, fields + 1, cap, width)] * chips + [jax.ShapeDtypeStruct((2, row_total), jnp.int32)],
        [(2, row_total, (fields + 1) * width), (chips, lats, fields + 1, cap, width)],
    )
    slot_back = over_chips(slot_back)
    (far,) = call(
        hold_kernel, dims, (me, far), [packed.shape], [pltpu.SemaphoreType.DMA(())], after=[dests, near]
    )
    states = [packed, near]
    for j in range(2, lats):
        if j % 2 == 0:
            states.append(far if j == 2 else swap(packed, "lat", j, lats))
        else:
            states.append(swap(states[j - 1], "lat", 1, lats))
    soon = [j for j in range(lats) if j == 2]
    late = [j for j in range(lats) if j != 2]
    message = (fields + 1, slabs, cap, width)
    sorted_soon = call(functools.partial(sort_kernel, soon), dims, (me, *slot_back), [message] * len(soon))
    mixed = call(
        mix_kernel,
        dims,
        (me, *slot_back, *states),
        [(2, lats, fields, cap, width)] * chips,
        [(lats, slabs, cap, width), (slabs, fields, cap, width)],
        after=sorted_soon,
    )
    sorted_late = call(
        functools.partial(sort_kernel, late), dims, (me, *slot_back), [message] * len(late), after=mixed[:1]
    )
    returned = [None] * lats
    for j, sorted_back in zip(soon + late, [*sorted_soon, *sorted_late]):
        returned[j] = sorted_back if j == 0 else swap(sorted_back, "lat", j, lats)
    moved = call(
        arrive_kernel,
        dims,
        (me, dests, *over_chips(mixed)),
        [(fields, 2, span, width)] * chips,
        [(fields, lats * chips, cap, width), (chips, fields, span, width)],
        after=returned[2:3],
    )
    tangent, tangent_pair = call(
        diffuse_kernel,
        dims,
        (me, inverse, *over_chips(moved)),
        [cot.shape, cot.shape],
        [(fields, levels * 2 * here, width)],
        after=returned[1:2] + returned[3:],
    )
    (adjoint,) = call(
        add_kernel,
        dims,
        (me, packed, *returned),
        [(lev_dev, fields, blocks, width)],
        after=[tangent_pair],
    )
    tangent = tangent + pair(tangent_pair)
    tangent_out = tangent.reshape(1, levels, fields, here, width).transpose(0, 1, 3, 2, 4)
    adjoint_out = adjoint.transpose(0, 2, 1, 3)[None]
    return tangent_out, adjoint_out


def solution(mesh):
    placed = (
        P("lat", "slab", None, None, None),
        P("lat", None, "slab", None, None),
        P("lat", "slab", None, None),
        P("lat", None, None, None),
        P("lat", "slab", None, None, None),
        P("lat", "slab", None),
    )
    return jax.shard_map(
        functools.partial(body, mesh.shape["lat"], mesh.shape["slab"]),
        mesh=mesh,
        in_specs=placed,
        out_specs=(P("lat", None, "slab", None, None), P("lat", "slab", None, None, None)),
        check_vma=False,
    )
```

```python
import functools

import jax
import jax.numpy as jnp
from jax import lax
from jax.experimental import pallas as pl
from jax.experimental.pallas import tpu as pltpu
from jax.sharding import PartitionSpec as P

LANES = 128
F32 = jnp.float32
EXACT = functools.partial(lax.dot_general, precision=lax.Precision.HIGHEST, preferred_element_type=F32)
SHORT = functools.partial(lax.dot_general, preferred_element_type=F32)


def two_parts(values):
    high = values.astype(jnp.bfloat16)
    return high, (values - high.astype(F32)).astype(jnp.bfloat16)


def pick(table, values, contract):
    dims = ((contract, (0,)), ((), ()))
    high, low = two_parts(values)
    return SHORT(table, low, dims) + SHORT(table, high, dims)


def product(left, right, contract):
    dims = ((contract, (0,)), ((), ()))
    left_high, left_low = two_parts(left)
    right_high, right_low = two_parts(right)
    return (
        SHORT(left_low, right_high, dims)
        + SHORT(left_high, right_low, dims)
        + SHORT(left_high, right_high, dims)
    )


def hot(rows, wanted):
    return jnp.where(rows == wanted, 1.0, 0.0).astype(jnp.bfloat16)


def iota(shape, axis):
    return lax.broadcasted_iota(jnp.int32, shape, axis)


def xor(a, b):
    return jnp.bitwise_xor(a, b)


def pack_kernel(dims, state, source_in, dest_in, cot_in, weight_in, inverse_in, *rest):
    lats, slabs, chips, cap, lev_dev, here, fields = dims
    out, mine, cot, weight, inverse, source, dest, sems = rest
    total = state.shape[0]
    copies = [
        pltpu.make_async_copy(src, dst, sems.at[i])
        for i, (src, dst) in enumerate(
            (
                (source_in, source),
                (dest_in, dest),
                (state, out.at[pl.ds(0, total)]),
                (cot_in, cot),
                (weight_in, weight),
                (inverse_in, inverse),
            )
        )
    ]
    for copy in copies:
        copy.start()
    copies[0].wait()
    copies[1].wait()
    numbers = source[...].reshape(lats * slabs, cap).astype(F32)
    slots = slabs * cap
    row = iota((slabs, slots), 0)
    at = iota((slabs, slots), 1)
    core = at // (chips * cap)
    chosen = row == (at // cap - core * chips) * 2 + core
    spread = jnp.where(iota((cap, slots), 1) % cap == iota((cap, slots), 0), 1.0, 0.0)
    wide = EXACT(numbers, spread, (((1,), (0,)), ((), ())))
    out[total:, :] = jnp.zeros((out.shape[0] - total, LANES), F32)
    for g in range(lats):
        lanes = jnp.where(chosen, wide[g * slabs : (g + 1) * slabs], 0.0)
        out[total + g : total + g + 1, :slots] = jnp.sum(lanes, axis=0, keepdims=True)
    slots = lats * chips * cap
    row = iota((lats * slabs, slots), 0)
    at = iota((lats * slabs, slots), 1)
    spread = jnp.where(iota((cap, slots), 1) % cap == iota((cap, slots), 0), 1.0, 0.0)
    wide = EXACT(numbers, spread, (((1,), (0,)), ((), ())))
    mine[...] = jnp.zeros(mine.shape, F32)
    for core in range(2):
        lanes = jnp.where(row == at // cap * 2 + core, wide, 0.0)
        mine[core : core + 1, :slots] = jnp.sum(lanes, axis=0, keepdims=True)
    mine[2:3, : dest.shape[1]] = dest[...].astype(F32)
    for copy in copies[2:]:
        copy.wait()


def start_kernel(dims, me, cot, inverse, cot_pair, weight, mine, *rest):
    lats, slabs, chips, cap, lev_dev, here, fields = dims
    out, back, held = rest[:chips], rest[-2], rest[-1]
    chip, core = me[1], me[2]
    levels = slabs * lev_dev
    step = fields * here
    span = lev_dev * 2 * here
    per = lats * cap
    for f in range(fields):
        own = [cot[pl.ds(f * here + b, levels, stride=step), :] for b in range(here)]
        pair = [cot_pair[pl.ds(f * here + b, levels, stride=step), :] for b in range(here)]
        own, pair = jnp.concatenate(own, axis=1), jnp.concatenate(pair, axis=1)
        wide = jnp.concatenate(
            [jnp.where(core == 0, own, pair), jnp.where(core == 0, pair, own)], axis=1
        )
        res = product(inverse[f], wide, (0,))
        for b in range(2 * here):
            back[f, pl.ds(b, levels, stride=2 * here), :] = res[:, b * LANES : (b + 1) * LANES]
    dest = mine[2:3, : weight.shape[0]].astype(jnp.int32)
    for x in range(2):
        res = pick(slot_table(dims, x, dest, True), weight[...], (1,))
        for c in range(chips):
            held[c, x] = res[c * per : (c + 1) * per]
    for k in range(chips):
        to = xor(chip, k)
        first = pl.multiple_of((to * 2 + core) * span, span)
        for f in range(fields):
            out[k][f * span : (f + 1) * span] = back[f, pl.ds(first, span), :]
        for x in range(2):
            at = fields * span + x * per
            out[k][at : at + per] = held[to, x]


def by_column_owner(dest, lev_dev, chips, wide):
    total = dest.shape[1]
    at = iota((total, total), 1)
    span = lev_dev * wide
    chip = at // span
    level = (at - chip * span) // wide
    block = at - chip * span - level * wide
    order = jnp.where(iota((total, total), 0) == (level * chips + chip) * wide + block, 1.0, 0.0)
    return EXACT(dest.astype(F32), order, (((1,), (0,)), ((), ()))).astype(jnp.int32)


def slot_table(dims, core, dest, by_chip):
    lats, slabs, chips, cap, lev_dev, here, fields = dims
    at = iota((lats * chips * cap, dest.shape[1]), 0)
    if by_chip:
        chip = at // (lats * cap)
        lat = at // cap - chip * lats
    else:
        lat = at // (chips * cap)
        chip = at // cap - lat * chips
    slot = at - at // cap * cap
    return hot(lat * (slabs * cap) + (chip * 2 + core) * cap + slot, dest)


def back_kernel(dims, me, mine, weight, *rest):
    lats, slabs, chips, cap, lev_dev, here, fields = dims
    got, out, other = rest[:chips], rest[-chips - 3 : -3], rest[-3]
    rows, slots = rest[-2:]
    chip, core = me[1], me[2]
    wide = 2 * here
    span = lev_dev * wide
    per = lats * cap
    order = by_column_owner(mine[2:3, : weight.shape[0]], lev_dev, chips, wide)
    for k in range(chips):
        first = pl.multiple_of(xor(chip, k) * span, span)
        for f in range(fields):
            rows[pl.ds(first, span), f * LANES : (f + 1) * LANES] = got[k][f * span : (f + 1) * span]
        other[xor(chip, k)] = got[k][pl.ds(pl.multiple_of(fields * span + (1 - core) * per, 8), per), :]
    for c in range(chips):
        for l in range(lev_dev):
            at = l * chips * wide + c * wide
            rows[c * span + l * wide : c * span + (l + 1) * wide, fields * LANES :] = weight[at : at + wide]
    tables = [slot_table(dims, core, order, False) for core in range(2)]
    res = pick(jnp.concatenate(tables, axis=0), rows[...], (1,))
    for core in range(2):
        for g in range(lats):
            for c in range(chips):
                at = ((core * lats + g) * chips + c) * cap
                for f in range(fields + 1):
                    slots[c, core, g, f] = res[at : at + cap, f * LANES : (f + 1) * LANES]
    for k in range(chips):
        out[k][...] = slots[xor(chip, k)]


def sort_kernel(groups, dims, me, *rest):
    lats, slabs, chips, cap, lev_dev, here, fields = dims
    got, outs = rest[:chips], rest[-len(groups) :]
    lat, chip, core = me[0], me[1], me[2]
    for k in range(chips):
        src = xor(chip, k)
        for out, j in zip(outs, groups):
            for x in range(2):
                for f in range(fields + 1):
                    out[f, x, src] = got[k][x, xor(lat, j), f]


def add_kernel(dims, me, mine, mine_pair, *rest):
    lats, slabs, chips, cap, lev_dev, here, fields = dims
    got, outs, rows = rest[:lats], rest[-3:-1], rest[-1]
    blocks = slabs * here
    row_total = lev_dev * blocks
    slots = lats * chips * cap
    lat, core = me[0], me[2]
    row = iota((row_total, slots), 0)
    for x, (source, out) in enumerate(zip((mine, mine_pair), outs)):
        for j in range(lats):
            for f in range(fields + 1):
                rows[f, xor(lat, j)] = got[j][f, xor(core, x)]
        low = source[pl.ds(core, 1), :slots].astype(jnp.int32)
        scale = jnp.concatenate([rows[fields].reshape(slots, LANES)] * fields, axis=1)
        value = jnp.concatenate([rows[f].reshape(slots, LANES) for f in range(fields)], axis=1)
        values = jnp.concatenate([(1.0 - scale) * value, scale * value], axis=0)
        table = jnp.concatenate([hot(row, low), hot(row, low + blocks)], axis=1)
        total = pick(table, values, (1,))
        for l in range(lev_dev):
            for f in range(fields):
                out[l, f] = total[l * blocks : (l + 1) * blocks, f * LANES : (f + 1) * LANES]


def hold_kernel(dims, me, array, mine, mine_pair, *rest):
    lats, slabs, chips, cap, lev_dev, here, fields = dims
    out, second, dests, sems = rest[-4:]
    cut = out.shape[0]
    copies = [
        pltpu.make_async_copy(array.at[pl.ds(0, cut)], out, sems.at[0]),
        pltpu.make_async_copy(array.at[pl.ds(cut, second.shape[0])], second, sems.at[1]),
    ]
    for copy in copies:
        copy.start()
    total = dests.shape[1]
    both = jnp.concatenate([mine[2:3, :total], mine_pair[2:3, :total]], axis=0)
    dests[...] = by_column_owner(both, lev_dev, chips, 2 * here)
    for copy in copies:
        copy.wait()


def mix_kernel(dims, me, weight_pair, *rest):
    lats, slabs, chips, cap, lev_dev, here, fields = dims
    got, packed, at = rest[:chips], [], chips
    for j in range(lats):
        count = 2 if forwarded(j) else 1
        packed.append(rest[at : at + count])
        at += count
    out, weight, mixed = rest[-chips - 2 : -2], rest[-2], rest[-1]
    lat, chip, core = me[0], me[1], me[2]
    blocks = slabs * here
    row_total = lev_dev * blocks
    slots = slabs * cap
    for g in range(lats):
        for k in range(chips):
            at = pl.multiple_of(fields * lev_dev * 2 * here + core * lats * cap, 8) + g * cap
            weight[g, core, xor(chip, k)] = got[k][pl.ds(at, cap), :]
            weight[g, 1 - core, k] = weight_pair[k, g * cap : (g + 1) * cap]
    row = iota((row_total, slots), 0)
    for j in range(lats):
        sender = xor(lat, j)
        tail = fields * row_total - sum(part.shape[0] for part in packed[j][:-1])
        low = packed[j][-1][pl.ds(tail + lat, 1), :][:, :slots].astype(jnp.int32)

        def level_rows(l, f, parts=packed[j]):
            at = (l * fields + f) * blocks
            if at >= parts[0].shape[0]:
                return parts[1][at - parts[0].shape[0] : at - parts[0].shape[0] + blocks]
            return parts[0][at : at + blocks]

        values = jnp.concatenate(
            [
                jnp.concatenate([level_rows(l, f) for l in range(lev_dev)], axis=0)
                for f in range(fields)
            ],
            axis=1,
        )
        table = jnp.concatenate([hot(row, low), hot(row, low + blocks)], axis=1)
        both = pick(table, values, (0,))
        scale = jnp.concatenate([weight[sender].reshape(slots, LANES)] * fields, axis=1)
        res = (1.0 - scale) * both[:slots] + scale * both[slots:]
        for r in range(2):
            for c in range(chips):
                at = (r * chips + c) * cap
                for f in range(fields):
                    mixed[r, c, f] = res[at : at + cap, f * LANES : (f + 1) * LANES]
        for k in range(chips):
            for x in range(2):
                out[k][x, sender] = mixed[xor(core, x), xor(chip, k)]


def arrive_kernel(dims, me, dest, *rest):
    lats, slabs, chips, cap, lev_dev, here, fields = dims
    got, out = rest[:chips], rest[-chips - 2 : -2]
    rows, moved = rest[-2:]
    chip, core = me[1], me[2]
    span = lev_dev * 2 * here
    for x in range(2):
        for k in range(chips):
            for g in range(lats):
                for f in range(fields):
                    rows[f, g * chips + xor(chip, k)] = got[k][x, g, f]
        values = jnp.concatenate(
            [rows[f].reshape(lats * chips * cap, LANES) for f in range(fields)], axis=1
        )
        res = pick(slot_table(dims, core, dest[x : x + 1, :], False), values, (0,))
        for c in range(chips):
            for f in range(fields):
                moved[c, f] = res[c * span : (c + 1) * span, f * LANES : (f + 1) * LANES]
        for k in range(chips):
            for f in range(fields):
                out[k][f, xor(core, x)] = moved[xor(chip, k), f]


def diffuse_kernel(dims, me, inverse, *rest):
    lats, slabs, chips, cap, lev_dev, here, fields = dims
    got, own, pair, rows = rest[:chips], rest[-3], rest[-2], rest[-1]
    chip, core = me[1], me[2]
    wide = 2 * here
    span = 2 * lev_dev * wide
    levels = slabs * lev_dev
    for k in range(chips):
        first = pl.multiple_of(xor(chip, k) * span, span)
        for f in range(fields):
            rows[f, pl.ds(first, span), :] = got[k][f].reshape(span, LANES)
    for f in range(fields):
        values = jnp.concatenate([rows[f, pl.ds(b, levels, stride=wide), :] for b in range(wide)], axis=1)
        res = product(inverse[f], values, (1,))
        first, second = res[:, : here * LANES], res[:, here * LANES :]
        mine, other = jnp.where(core == 0, first, second), jnp.where(core == 0, second, first)
        for b in range(here):
            at = pl.ds(f * here + b, levels, stride=fields * here)
            own[at, :] = mine[:, b * LANES : (b + 1) * LANES]
            pair[at, :] = other[:, b * LANES : (b + 1) * LANES]


def call(kernel, dims, args, outs, scratch=(), after=(), outside=False, limit=48):
    inside = pl.BlockSpec(memory_space=pltpu.VMEM)
    anywhere = pl.BlockSpec(memory_space=pl.ANY)
    if outside:
        specs = [anywhere] * len(args)
    else:
        specs = [pl.BlockSpec(memory_space=pltpu.SMEM)] + [inside] * (len(args) - 1)
    return pl.pallas_call(
        functools.partial(kernel, dims),
        out_shape=[shape if hasattr(shape, "dtype") else jax.ShapeDtypeStruct(shape, F32) for shape in outs],
        in_specs=specs + [anywhere] * len(after),
        out_specs=[inside] * len(outs),
        scratch_shapes=[pltpu.VMEM(shape, F32) if isinstance(shape, tuple) else shape for shape in scratch],
        compiler_params=pltpu.CompilerParams(vmem_limit_bytes=limit * 1024 * 1024),
    )(*args, *after)


def forwarded(j):
    return j % 2 == 1 and j > 1


def swap(array, axis, bit, count):
    return lax.ppermute(array, axis, [(i, i ^ bit) for i in range(count)])


def body(lats, slabs, field_state, cotangent, vertical_weight, diffusion_inverse, source_row, dest_slot):
    _, lev_dev, blocks, fields, width = field_state.shape
    cap = source_row.shape[-1]
    chips = slabs // 2
    here = blocks // slabs
    levels = slabs * lev_dev
    row_total = lev_dev * blocks
    span = lev_dev * 2 * here
    dims = (lats, slabs, chips, cap, lev_dev, here, fields)
    lat, slab = lax.axis_index("lat"), lax.axis_index("slab")
    me = jnp.stack([lat, slab // 2, slab % 2]).astype(jnp.int32)

    def pair(array):
        return swap(array, "slab", 1, slabs)

    def over_chips(messages):
        got = list(messages)
        for k in reversed(range(1, chips)):
            got[k] = swap(messages[k], "slab", 2 * k, slabs)
        return got

    state = field_state[0].transpose(0, 2, 1, 3).reshape(row_total * fields, width)
    cot = cotangent[0].transpose(0, 2, 1, 3).reshape(levels * fields * here, width)
    weights = vertical_weight.reshape(row_total, width)
    inverse = diffusion_inverse[0]
    dest = dest_slot[0]

    packed, mine, cot_here, weights_here, inverse_here = call(
        pack_kernel,
        dims,
        [
            pltpu.with_memory_space_constraint(array, pltpu.HBM)
            for array in (state, source_row[0, 0], dest, cot, weights, inverse)
        ],
        [
            (row_total * fields + -(-lats // 8) * 8, width),
            (8, max(row_total, lats * chips * cap)),
            cot.shape,
            weights.shape,
            inverse.shape,
        ],
        [
            pltpu.VMEM((lats, slabs, cap), jnp.int32),
            pltpu.VMEM(dest.shape, jnp.int32),
            pltpu.SemaphoreType.DMA((6,)),
        ],
        outside=True,
        limit=48,
    )
    mine_pair = pair(mine)
    near, far = swap(packed, "lat", 1, lats), swap(packed, "lat", 2, lats)
    first = over_chips(
        call(
            start_kernel,
            dims,
            (me, cot_here, inverse_here, pair(cot), weights_here, mine),
            [(fields * span + 2 * lats * cap, width)] * chips,
            [(fields, levels * 2 * here, width), (chips, 2, lats * cap, width)],
        )
    )
    *slot_back, weight_other = call(
        back_kernel,
        dims,
        (me, mine, weights_here, *first),
        [(2, lats, fields + 1, cap, width)] * chips + [(chips, lats * cap, width)],
        [(row_total, (fields + 1) * width), (chips, 2, lats, fields + 1, cap, width)],
        after=[mine_pair],
    )
    cut = row_total * fields // 2
    first_half, second_half, dests = call(
        hold_kernel,
        dims,
        (me, far, mine, mine_pair),
        [(cut, width), (packed.shape[0] - cut, width), jax.ShapeDtypeStruct((2, row_total), jnp.int32)],
        [pltpu.SemaphoreType.DMA((2,))],
        after=[slot_back[0], near],
    )
    slot_back = over_chips(slot_back)
    states = []
    for j in range(lats):
        if forwarded(j):
            halves = (first_half, second_half) if j == 3 else (states[-1][:cut], states[-1][cut:])
            states += [swap(half, "lat", 1, lats) for half in halves]
        else:
            states.append({0: packed, 1: near, 2: far}[j] if j < 3 else swap(packed, "lat", j, lats))
    mixed = call(
        mix_kernel,
        dims,
        (me, pair(weight_other), *first, *states),
        [(2, lats, fields, cap, width)] * chips,
        [(lats, 2, chips, cap, width), (2, chips, fields, cap, width)],
    )
    soon = [j for j in range(lats) if j == 2]
    late = [j for j in range(lats) if j not in (1, 2)]
    message = (fields + 1, 2, chips, cap, width)
    sorted_soon = call(functools.partial(sort_kernel, soon), dims, (me, *slot_back), [message] * len(soon))
    sorted_late = call(
        functools.partial(sort_kernel, late), dims, (me, *slot_back), [message] * len(late), after=mixed[:1]
    )
    returned = [None] * lats
    for j, sorted_back in zip(soon + late, [*sorted_soon, *sorted_late]):
        returned[j] = sorted_back if j == 0 else swap(sorted_back, "lat", j, lats)
    moved = call(
        arrive_kernel,
        dims,
        (me, dests, *over_chips(mixed)),
        [(fields, 2, span, width)] * chips,
        [(fields, lats * chips, cap, width), (chips, fields, span, width)],
        after=returned[2:3],
    )
    (sorted_last,) = call(
        functools.partial(sort_kernel, [1]), dims, (me, *slot_back), [message], after=moved[:1]
    )
    returned[1] = swap(sorted_last, "lat", 1, lats)
    tangent, tangent_pair = call(
        diffuse_kernel,
        dims,
        (me, inverse_here, *over_chips(moved)),
        [cot.shape, cot.shape],
        [(fields, levels * 2 * here, width)],
        after=returned[3:4],
    )
    adjoint, adjoint_pair = call(
        add_kernel,
        dims,
        (me, mine, mine_pair, *returned),
        [(lev_dev, fields, blocks, width)] * 2,
        [(fields + 1, lats, chips, cap, width)],
        after=[tangent_pair],
    )
    adjoint = adjoint + pair(adjoint_pair)
    tangent = tangent + pair(tangent_pair)
    tangent_out = tangent.reshape(1, levels, fields, here, width).transpose(0, 1, 3, 2, 4)
    adjoint_out = adjoint.transpose(0, 2, 1, 3)[None]
    return tangent_out, adjoint_out


def solution(mesh):
    placed = (
        P("lat", "slab", None, None, None),
        P("lat", None, "slab", None, None),
        P("lat", "slab", None, None),
        P("lat", None, None, None),
        P("lat", "slab", None, None, None),
        P("lat", "slab", None),
    )
    return jax.shard_map(
        functools.partial(body, mesh.shape["lat"], mesh.shape["slab"]),
        mesh=mesh,
        in_specs=placed,
        out_specs=(P("lat", None, "slab", None, None), P("lat", "slab", None, None, None)),
        check_vma=False,
    )
```

```python
import functools

import jax
import jax.numpy as jnp
from jax import lax
from jax.experimental import pallas as pl
from jax.experimental.pallas import tpu as pltpu
from jax.sharding import PartitionSpec as P

LANES = 128
F32 = jnp.float32
EXACT = functools.partial(lax.dot_general, precision=lax.Precision.HIGHEST, preferred_element_type=F32)
SHORT = functools.partial(lax.dot_general, preferred_element_type=F32)


def two_parts(values):
    high = values.astype(jnp.bfloat16)
    return high, (values - high.astype(F32)).astype(jnp.bfloat16)


def pick(table, values, contract):
    table = jnp.concatenate([table, table], axis=contract[0])
    return SHORT(table, jnp.concatenate(two_parts(values), axis=0), ((contract, (0,)), ((), ())))


def product(left, right, contract):
    left_high, left_low = two_parts(left)
    right_high, right_low = two_parts(right)
    left = jnp.concatenate([left_high, left_low, left_high], axis=contract[0])
    right = jnp.concatenate([right_high, right_high, right_low], axis=0)
    return SHORT(left, right, ((contract, (0,)), ((), ())))


def hot(rows, wanted):
    return jnp.where(rows == wanted, 1.0, 0.0).astype(jnp.bfloat16)


def iota(shape, axis):
    return lax.broadcasted_iota(jnp.int32, shape, axis)


def xor(a, b):
    return jnp.bitwise_xor(a, b)


def pack_kernel(dims, state, source_in, dest_in, cot_in, weight_in, inverse_in, *rest):
    lats, slabs, chips, cap, lev_dev, here, fields = dims
    out, second_half, mine, cot, weight, inverse, source, dest, sems = rest
    total = state.shape[0]
    cut = out.shape[0] - second_half.shape[0]
    copies = [
        pltpu.make_async_copy(src, dst, sems.at[i])
        for i, (src, dst) in enumerate(
            (
                (source_in, source),
                (dest_in, dest),
                (state, out.at[pl.ds(0, total)]),
                (state.at[pl.ds(cut, total - cut)], second_half.at[pl.ds(0, total - cut)]),
                (cot_in, cot),
                (weight_in, weight),
                (inverse_in, inverse),
            )
        )
    ]
    for copy in copies:
        copy.start()
    copies[0].wait()
    copies[1].wait()
    numbers = source[...].reshape(lats * slabs, cap).astype(F32)
    slots = slabs * cap
    row = iota((slabs, slots), 0)
    at = iota((slabs, slots), 1)
    core = at // (chips * cap)
    chosen = row == (at // cap - core * chips) * 2 + core
    spread = jnp.where(iota((cap, slots), 1) % cap == iota((cap, slots), 0), 1.0, 0.0)
    wide = EXACT(numbers, spread, (((1,), (0,)), ((), ())))
    out[total:, :] = jnp.zeros((out.shape[0] - total, LANES), F32)
    for g in range(lats):
        lanes = jnp.where(chosen, wide[g * slabs : (g + 1) * slabs], 0.0)
        out[total + g : total + g + 1, :slots] = jnp.sum(lanes, axis=0, keepdims=True)
    second_half[total - cut :, :] = out[total:, :]
    slots = lats * chips * cap
    row = iota((lats * slabs, slots), 0)
    at = iota((lats * slabs, slots), 1)
    spread = jnp.where(iota((cap, slots), 1) % cap == iota((cap, slots), 0), 1.0, 0.0)
    wide = EXACT(numbers, spread, (((1,), (0,)), ((), ())))
    mine[...] = jnp.zeros(mine.shape, F32)
    for core in range(2):
        lanes = jnp.where(row == at // cap * 2 + core, wide, 0.0)
        mine[core : core + 1, :slots] = jnp.sum(lanes, axis=0, keepdims=True)
    mine[2:3, : dest.shape[1]] = dest[...].astype(F32)
    for copy in copies[2:]:
        copy.wait()


def start_kernel(dims, me, cot, inverse, cot_pair, weight, mine, *rest):
    lats, slabs, chips, cap, lev_dev, here, fields = dims
    out, back, held = rest[:chips], rest[-2], rest[-1]
    chip, core = me[1], me[2]
    levels = slabs * lev_dev
    step = fields * here
    span = lev_dev * 2 * here
    per = lats * cap
    for f in range(fields):
        own = [cot[pl.ds(f * here + b, levels, stride=step), :] for b in range(here)]
        pair = [cot_pair[pl.ds(f * here + b, levels, stride=step), :] for b in range(here)]
        own, pair = jnp.concatenate(own, axis=1), jnp.concatenate(pair, axis=1)
        wide = jnp.concatenate(
            [jnp.where(core == 0, own, pair), jnp.where(core == 0, pair, own)], axis=1
        )
        res = product(inverse[f], wide, (0,))
        for b in range(2 * here):
            back[f, pl.ds(b, levels, stride=2 * here), :] = res[:, b * LANES : (b + 1) * LANES]
    dest = mine[2:3, : weight.shape[0]].astype(jnp.int32)
    for x in range(2):
        res = pick(slot_table(dims, x, dest, True), weight[...], (1,))
        for c in range(chips):
            held[c, x] = res[c * per : (c + 1) * per]
    for k in range(chips):
        to = xor(chip, k)
        first = pl.multiple_of((to * 2 + core) * span, span)
        for f in range(fields):
            out[k][f * span : (f + 1) * span] = back[f, pl.ds(first, span), :]
        for x in range(2):
            at = fields * span + x * per
            out[k][at : at + per] = held[to, x]


def by_column_owner(dest, lev_dev, chips, wide):
    total = dest.shape[1]
    at = iota((total, total), 1)
    span = lev_dev * wide
    chip = at // span
    level = (at - chip * span) // wide
    block = at - chip * span - level * wide
    order = jnp.where(iota((total, total), 0) == (level * chips + chip) * wide + block, 1.0, 0.0)
    return EXACT(dest.astype(F32), order, (((1,), (0,)), ((), ()))).astype(jnp.int32)


def slot_table(dims, core, dest, by_chip):
    lats, slabs, chips, cap, lev_dev, here, fields = dims
    at = iota((lats * chips * cap, dest.shape[1]), 0)
    if by_chip:
        chip = at // (lats * cap)
        lat = at // cap - chip * lats
    else:
        lat = at // (chips * cap)
        chip = at // cap - lat * chips
    slot = at - at // cap * cap
    return hot(lat * (slabs * cap) + (chip * 2 + core) * cap + slot, dest)


def back_kernel(dims, me, mine, weight, *rest):
    lats, slabs, chips, cap, lev_dev, here, fields = dims
    got, out, other = rest[:chips], rest[-chips - 3 : -3], rest[-3]
    rows, slots = rest[-2:]
    chip, core = me[1], me[2]
    wide = 2 * here
    span = lev_dev * wide
    per = lats * cap
    order = by_column_owner(mine[2:3, : weight.shape[0]], lev_dev, chips, wide)
    for k in range(chips):
        first = pl.multiple_of(xor(chip, k) * span, span)
        for f in range(fields):
            rows[pl.ds(first, span), f * LANES : (f + 1) * LANES] = got[k][f * span : (f + 1) * span]
        other[xor(chip, k)] = got[k][pl.ds(pl.multiple_of(fields * span + (1 - core) * per, 8), per), :]
    for c in range(chips):
        for l in range(lev_dev):
            at = l * chips * wide + c * wide
            rows[c * span + l * wide : c * span + (l + 1) * wide, fields * LANES :] = weight[at : at + wide]
    tables = [slot_table(dims, core, order, False) for core in range(2)]
    res = pick(jnp.concatenate(tables, axis=0), rows[...], (1,))
    for core in range(2):
        for g in range(lats):
            for c in range(chips):
                at = ((core * lats + g) * chips + c) * cap
                for f in range(fields + 1):
                    slots[c, core, g, f] = res[at : at + cap, f * LANES : (f + 1) * LANES]
    for k in range(chips):
        out[k][...] = slots[xor(chip, k)]


def sort_kernel(groups, dims, me, *rest):
    lats, slabs, chips, cap, lev_dev, here, fields = dims
    got, outs = rest[:chips], rest[-len(groups) :]
    lat, chip, core = me[0], me[1], me[2]
    for k in range(chips):
        src = xor(chip, k)
        for out, j in zip(outs, groups):
            for x in range(2):
                for f in range(fields + 1):
                    out[f, x, src] = got[k][x, xor(lat, j), f]


def add_kernel(dims, me, mine, mine_pair, *rest):
    lats, slabs, chips, cap, lev_dev, here, fields = dims
    got, outs, rows = rest[:lats], rest[-3:-1], rest[-1]
    blocks = slabs * here
    row_total = lev_dev * blocks
    slots = lats * chips * cap
    lat, core = me[0], me[2]
    row = iota((row_total, slots), 0)
    for x, (source, out) in enumerate(zip((mine, mine_pair), outs)):
        for j in range(lats):
            for f in range(fields + 1):
                rows[f, xor(lat, j)] = got[j][f, xor(core, x)]
        low = source[pl.ds(core, 1), :slots].astype(jnp.int32)
        scale = jnp.concatenate([rows[fields].reshape(slots, LANES)] * fields, axis=1)
        value = jnp.concatenate([rows[f].reshape(slots, LANES) for f in range(fields)], axis=1)
        values = jnp.concatenate([(1.0 - scale) * value, scale * value], axis=0)
        table = jnp.concatenate([hot(row, low), hot(row, low + blocks)], axis=1)
        total = pick(table, values, (1,))
        for l in range(lev_dev):
            for f in range(fields):
                out[l, f] = total[l * blocks : (l + 1) * blocks, f * LANES : (f + 1) * LANES]


def hold_kernel(dims, me, array, mine, mine_pair, *rest):
    lats, slabs, chips, cap, lev_dev, here, fields = dims
    out, dests, sem = rest[-3:]
    copy = pltpu.make_async_copy(array.at[pl.ds(0, out.shape[0])], out, sem)
    copy.start()
    total = dests.shape[1]
    both = jnp.concatenate([mine[2:3, :total], mine_pair[2:3, :total]], axis=0)
    dests[...] = by_column_owner(both, lev_dev, chips, 2 * here)
    copy.wait()


def mix_kernel(dims, me, weight_pair, *rest):
    lats, slabs, chips, cap, lev_dev, here, fields = dims
    got, packed, at = rest[:chips], [], chips
    for j in range(lats):
        count = 2 if forwarded(j) else 1
        packed.append(rest[at : at + count])
        at += count
    out, weight, mixed = rest[-chips - 2 : -2], rest[-2], rest[-1]
    lat, chip, core = me[0], me[1], me[2]
    blocks = slabs * here
    row_total = lev_dev * blocks
    slots = slabs * cap
    for g in range(lats):
        for k in range(chips):
            at = pl.multiple_of(fields * lev_dev * 2 * here + core * lats * cap, 8) + g * cap
            weight[g, core, xor(chip, k)] = got[k][pl.ds(at, cap), :]
            weight[g, 1 - core, k] = weight_pair[k, g * cap : (g + 1) * cap]
    row = iota((row_total, slots), 0)
    for j in range(lats):
        sender = xor(lat, j)
        tail = fields * row_total - sum(part.shape[0] for part in packed[j][:-1])
        low = packed[j][-1][pl.ds(tail + lat, 1), :][:, :slots].astype(jnp.int32)

        def level_rows(l, f, parts=packed[j]):
            at = (l * fields + f) * blocks
            if at >= parts[0].shape[0]:
                return parts[1][at - parts[0].shape[0] : at - parts[0].shape[0] + blocks]
            return parts[0][at : at + blocks]

        values = jnp.concatenate(
            [
                jnp.concatenate([level_rows(l, f) for l in range(lev_dev)], axis=0)
                for f in range(fields)
            ],
            axis=1,
        )
        table = jnp.concatenate([hot(row, low), hot(row, low + blocks)], axis=1)
        both = pick(table, values, (0,))
        scale = jnp.concatenate([weight[sender].reshape(slots, LANES)] * fields, axis=1)
        res = (1.0 - scale) * both[:slots] + scale * both[slots:]
        for r in range(2):
            for c in range(chips):
                at = (r * chips + c) * cap
                for f in range(fields):
                    mixed[r, c, f] = res[at : at + cap, f * LANES : (f + 1) * LANES]
        for k in range(chips):
            for x in range(2):
                out[k][x, sender] = mixed[xor(core, x), xor(chip, k)]


def arrive_kernel(dims, me, dest, *rest):
    lats, slabs, chips, cap, lev_dev, here, fields = dims
    got, out = rest[:chips], rest[-chips - 2 : -2]
    rows, moved = rest[-2:]
    chip, core = me[1], me[2]
    span = lev_dev * 2 * here
    for x in range(2):
        for k in range(chips):
            for g in range(lats):
                for f in range(fields):
                    rows[f, g * chips + xor(chip, k)] = got[k][x, g, f]
        values = jnp.concatenate(
            [rows[f].reshape(lats * chips * cap, LANES) for f in range(fields)], axis=1
        )
        res = pick(slot_table(dims, core, dest[x : x + 1, :], False), values, (0,))
        for c in range(chips):
            for f in range(fields):
                moved[c, f] = res[c * span : (c + 1) * span, f * LANES : (f + 1) * LANES]
        for k in range(chips):
            for f in range(fields):
                out[k][f, xor(core, x)] = moved[xor(chip, k), f]


def diffuse_kernel(dims, me, inverse, *rest):
    lats, slabs, chips, cap, lev_dev, here, fields = dims
    got, own, pair, rows = rest[:chips], rest[-3], rest[-2], rest[-1]
    chip, core = me[1], me[2]
    wide = 2 * here
    span = 2 * lev_dev * wide
    levels = slabs * lev_dev
    for k in range(chips):
        first = pl.multiple_of(xor(chip, k) * span, span)
        for f in range(fields):
            rows[f, pl.ds(first, span), :] = got[k][f].reshape(span, LANES)
    for f in range(fields):
        values = jnp.concatenate([rows[f, pl.ds(b, levels, stride=wide), :] for b in range(wide)], axis=1)
        res = product(inverse[f], values, (1,))
        first, second = res[:, : here * LANES], res[:, here * LANES :]
        mine, other = jnp.where(core == 0, first, second), jnp.where(core == 0, second, first)
        for b in range(here):
            at = pl.ds(f * here + b, levels, stride=fields * here)
            own[at, :] = mine[:, b * LANES : (b + 1) * LANES]
            pair[at, :] = other[:, b * LANES : (b + 1) * LANES]


def call(kernel, dims, args, outs, scratch=(), after=(), outside=False, limit=48):
    inside = pl.BlockSpec(memory_space=pltpu.VMEM)
    anywhere = pl.BlockSpec(memory_space=pl.ANY)
    if outside:
        specs = [anywhere] * len(args)
    else:
        specs = [pl.BlockSpec(memory_space=pltpu.SMEM)] + [inside] * (len(args) - 1)
    return pl.pallas_call(
        functools.partial(kernel, dims),
        out_shape=[shape if hasattr(shape, "dtype") else jax.ShapeDtypeStruct(shape, F32) for shape in outs],
        in_specs=specs + [anywhere] * len(after),
        out_specs=[inside] * len(outs),
        scratch_shapes=[pltpu.VMEM(shape, F32) if isinstance(shape, tuple) else shape for shape in scratch],
        compiler_params=pltpu.CompilerParams(vmem_limit_bytes=limit * 1024 * 1024),
    )(*args, *after)


def forwarded(j):
    return j % 2 == 1 and j > 1


def swap(array, axis, bit, count):
    return lax.ppermute(array, axis, [(i, i ^ bit) for i in range(count)])


def body(lats, slabs, field_state, cotangent, vertical_weight, diffusion_inverse, source_row, dest_slot):
    _, lev_dev, blocks, fields, width = field_state.shape
    cap = source_row.shape[-1]
    chips = slabs // 2
    here = blocks // slabs
    levels = slabs * lev_dev
    row_total = lev_dev * blocks
    span = lev_dev * 2 * here
    dims = (lats, slabs, chips, cap, lev_dev, here, fields)
    lat, slab = lax.axis_index("lat"), lax.axis_index("slab")
    me = jnp.stack([lat, slab // 2, slab % 2]).astype(jnp.int32)

    def pair(array):
        return swap(array, "slab", 1, slabs)

    def over_chips(messages):
        got = list(messages)
        for k in reversed(range(1, chips)):
            got[k] = swap(messages[k], "slab", 2 * k, slabs)
        return got

    state = field_state[0].transpose(0, 2, 1, 3).reshape(row_total * fields, width)
    cot = cotangent[0].transpose(0, 2, 1, 3).reshape(levels * fields * here, width)
    weights = vertical_weight.reshape(row_total, width)
    inverse = diffusion_inverse[0]
    dest = dest_slot[0]

    cut = row_total * fields // 2
    packed, second_half, mine, cot_here, weights_here, inverse_here = call(
        pack_kernel,
        dims,
        [
            pltpu.with_memory_space_constraint(array, pltpu.HBM)
            for array in (state, source_row[0, 0], dest, cot, weights, inverse)
        ],
        [
            (row_total * fields + -(-lats // 8) * 8, width),
            (row_total * fields + -(-lats // 8) * 8 - cut, width),
            (8, max(row_total, lats * chips * cap)),
            cot.shape,
            weights.shape,
            inverse.shape,
        ],
        [
            pltpu.VMEM((lats, slabs, cap), jnp.int32),
            pltpu.VMEM(dest.shape, jnp.int32),
            pltpu.SemaphoreType.DMA((7,)),
        ],
        outside=True,
        limit=48,
    )
    mine_pair = pair(mine)
    near, far = swap(packed, "lat", 1, lats), swap(packed, "lat", 2, lats)
    first = over_chips(
        call(
            start_kernel,
            dims,
            (me, cot_here, inverse_here, pair(cot), weights_here, mine),
            [(fields * span + 2 * lats * cap, width)] * chips,
            [(fields, levels * 2 * here, width), (chips, 2, lats * cap, width)],
        )
    )
    *slot_back, weight_other = call(
        back_kernel,
        dims,
        (me, mine, weights_here, *first),
        [(2, lats, fields + 1, cap, width)] * chips + [(chips, lats * cap, width)],
        [(row_total, (fields + 1) * width), (chips, 2, lats, fields + 1, cap, width)],
        after=[mine_pair],
    )
    opposite = swap(second_half, "lat", 3, lats)
    first_half, dests = call(
        hold_kernel,
        dims,
        (me, far, mine, mine_pair),
        [(cut, width), jax.ShapeDtypeStruct((2, row_total), jnp.int32)],
        [pltpu.SemaphoreType.DMA(())],
        after=[slot_back[0], near],
    )
    slot_back = over_chips(slot_back)
    states = []
    for j in range(lats):
        if forwarded(j):
            states.append(swap(first_half if j == 3 else states[-1][:cut], "lat", 1, lats))
            states.append(opposite if j == 3 else swap(second_half, "lat", j, lats))
        else:
            states.append({0: packed, 1: near, 2: far}[j] if j < 3 else swap(packed, "lat", j, lats))
    soon = [j for j in range(lats) if j == 2]
    late = [j for j in range(lats) if j != 2]
    message = (fields + 1, 2, chips, cap, width)
    sorted_soon = call(functools.partial(sort_kernel, soon), dims, (me, *slot_back), [message] * len(soon))
    mixed = call(
        mix_kernel,
        dims,
        (me, pair(weight_other), *first, *states),
        [(2, lats, fields, cap, width)] * chips,
        [(lats, 2, chips, cap, width), (2, chips, fields, cap, width)],
        after=sorted_soon,
    )
    sorted_late = call(
        functools.partial(sort_kernel, late), dims, (me, *slot_back), [message] * len(late), after=mixed[:1]
    )
    returned = [None] * lats
    for j, sorted_back in zip(soon + late, [*sorted_soon, *sorted_late]):
        returned[j] = sorted_back if j == 0 else swap(sorted_back, "lat", j, lats)
    moved = call(
        arrive_kernel,
        dims,
        (me, dests, *over_chips(mixed)),
        [(fields, 2, span, width)] * chips,
        [(fields, lats * chips, cap, width), (chips, fields, span, width)],
        after=returned[2:3],
    )
    moved = over_chips(moved)
    adjoint, adjoint_pair = call(
        add_kernel,
        dims,
        (me, mine, mine_pair, *returned),
        [(lev_dev, fields, blocks, width)] * 2,
        [(fields + 1, lats, chips, cap, width)],
        after=moved[1:2],
    )
    tangent, tangent_pair = call(
        diffuse_kernel,
        dims,
        (me, inverse_here, *moved),
        [cot.shape, cot.shape],
        [(fields, levels * 2 * here, width)],
        after=[adjoint_pair],
    )
    adjoint = adjoint + pair(adjoint_pair)
    tangent = tangent + pair(tangent_pair)
    tangent_out = tangent.reshape(1, levels, fields, here, width).transpose(0, 1, 3, 2, 4)
    adjoint_out = adjoint.transpose(0, 2, 1, 3)[None]
    return tangent_out, adjoint_out


def solution(mesh):
    placed = (
        P("lat", "slab", None, None, None),
        P("lat", None, "slab", None, None),
        P("lat", "slab", None, None),
        P("lat", None, None, None),
        P("lat", "slab", None, None, None),
        P("lat", "slab", None),
    )
    return jax.shard_map(
        functools.partial(body, mesh.shape["lat"], mesh.shape["slab"]),
        mesh=mesh,
        in_specs=placed,
        out_specs=(P("lat", None, "slab", None, None), P("lat", "slab", None, None, None)),
        check_vma=False,
    )
```

```python
import functools

import jax
import jax.numpy as jnp
from jax import lax
from jax.experimental import pallas as pl
from jax.experimental.pallas import tpu as pltpu
from jax.sharding import PartitionSpec as P

LANES = 128
F32 = jnp.float32
EXACT = functools.partial(lax.dot_general, precision=lax.Precision.HIGHEST, preferred_element_type=F32)
SHORT = functools.partial(lax.dot_general, preferred_element_type=F32)


def two_parts(values):
    high = values.astype(jnp.bfloat16)
    return high, (values - high.astype(F32)).astype(jnp.bfloat16)


def pick(table, values, contract):
    table = jnp.concatenate([table, table], axis=contract[0])
    return SHORT(table, jnp.concatenate(two_parts(values), axis=0), ((contract, (0,)), ((), ())))


def product(left, right, contract):
    left_high, left_low = two_parts(left)
    right_high, right_low = two_parts(right)
    left = jnp.concatenate([left_high, left_low, left_high], axis=contract[0])
    right = jnp.concatenate([right_high, right_high, right_low], axis=0)
    return SHORT(left, right, ((contract, (0,)), ((), ())))


def hot(rows, wanted):
    return jnp.where(rows == wanted, 1.0, 0.0).astype(jnp.bfloat16)


def iota(shape, axis):
    return lax.broadcasted_iota(jnp.int32, shape, axis)


def xor(a, b):
    return jnp.bitwise_xor(a, b)


def pack_kernel(dims, state, source_in, dest_in, cot_in, weight_in, inverse_in, *rest):
    lats, slabs, chips, cap, lev_dev, here, fields = dims
    out, second_half, mine, cot, weight, inverse, source, dest, sems = rest
    total = state.shape[0]
    cut = out.shape[0] - second_half.shape[0]
    copies = [
        pltpu.make_async_copy(src, dst, sems.at[i])
        for i, (src, dst) in enumerate(
            (
                (source_in, source),
                (dest_in, dest),
                (state, out.at[pl.ds(0, total)]),
                (state.at[pl.ds(cut, total - cut)], second_half.at[pl.ds(0, total - cut)]),
                (cot_in, cot),
                (weight_in, weight),
                (inverse_in, inverse),
            )
        )
    ]
    for copy in copies:
        copy.start()
    copies[0].wait()
    copies[1].wait()
    numbers = source[...].reshape(lats * slabs, cap).astype(F32)
    slots = slabs * cap
    row = iota((slabs, slots), 0)
    at = iota((slabs, slots), 1)
    core = at // (chips * cap)
    chosen = row == (at // cap - core * chips) * 2 + core
    spread = jnp.where(iota((cap, slots), 1) % cap == iota((cap, slots), 0), 1.0, 0.0)
    wide = EXACT(numbers, spread, (((1,), (0,)), ((), ())))
    out[total:, :] = jnp.zeros((out.shape[0] - total, LANES), F32)
    for g in range(lats):
        lanes = jnp.where(chosen, wide[g * slabs : (g + 1) * slabs], 0.0)
        out[total + g : total + g + 1, :slots] = jnp.sum(lanes, axis=0, keepdims=True)
    second_half[total - cut :, :] = out[total:, :]
    slots = lats * chips * cap
    row = iota((lats * slabs, slots), 0)
    at = iota((lats * slabs, slots), 1)
    spread = jnp.where(iota((cap, slots), 1) % cap == iota((cap, slots), 0), 1.0, 0.0)
    wide = EXACT(numbers, spread, (((1,), (0,)), ((), ())))
    mine[...] = jnp.zeros(mine.shape, F32)
    for core in range(2):
        lanes = jnp.where(row == at // cap * 2 + core, wide, 0.0)
        mine[core : core + 1, :slots] = jnp.sum(lanes, axis=0, keepdims=True)
    mine[2:3, : dest.shape[1]] = dest[...].astype(F32)
    for copy in copies[2:]:
        copy.wait()


def start_kernel(dims, me, cot, inverse, cot_pair, weight, mine, *rest):
    lats, slabs, chips, cap, lev_dev, here, fields = dims
    out, back, held = rest[:chips], rest[-2], rest[-1]
    chip, core = me[1], me[2]
    levels = slabs * lev_dev
    step = fields * here
    span = lev_dev * 2 * here
    per = lats * cap
    for f in range(fields):
        own = [cot[pl.ds(f * here + b, levels, stride=step), :] for b in range(here)]
        pair = [cot_pair[pl.ds(f * here + b, levels, stride=step), :] for b in range(here)]
        own, pair = jnp.concatenate(own, axis=1), jnp.concatenate(pair, axis=1)
        wide = jnp.concatenate(
            [jnp.where(core == 0, own, pair), jnp.where(core == 0, pair, own)], axis=1
        )
        res = product(inverse[f], wide, (0,))
        for b in range(2 * here):
            back[f, pl.ds(b, levels, stride=2 * here), :] = res[:, b * LANES : (b + 1) * LANES]
    dest = mine[2:3, : weight.shape[0]].astype(jnp.int32)
    for x in range(2):
        res = pick(slot_table(dims, x, dest, True), weight[...], (1,))
        for c in range(chips):
            held[c, x] = res[c * per : (c + 1) * per]
    for k in range(chips):
        to = xor(chip, k)
        first = pl.multiple_of((to * 2 + core) * span, span)
        for f in range(fields):
            out[k][f * span : (f + 1) * span] = back[f, pl.ds(first, span), :]
        for x in range(2):
            at = fields * span + x * per
            out[k][at : at + per] = held[to, x]


def by_column_owner(dest, lev_dev, chips, wide):
    total = dest.shape[1]
    at = iota((total, total), 1)
    span = lev_dev * wide
    chip = at // span
    level = (at - chip * span) // wide
    block = at - chip * span - level * wide
    order = jnp.where(iota((total, total), 0) == (level * chips + chip) * wide + block, 1.0, 0.0)
    return EXACT(dest.astype(F32), order, (((1,), (0,)), ((), ()))).astype(jnp.int32)


def slot_table(dims, core, dest, by_chip):
    lats, slabs, chips, cap, lev_dev, here, fields = dims
    at = iota((lats * chips * cap, dest.shape[1]), 0)
    if by_chip:
        chip = at // (lats * cap)
        lat = at // cap - chip * lats
    else:
        lat = at // (chips * cap)
        chip = at // cap - lat * chips
    slot = at - at // cap * cap
    return hot(lat * (slabs * cap) + (chip * 2 + core) * cap + slot, dest)


def back_kernel(dims, me, mine, weight, *rest):
    lats, slabs, chips, cap, lev_dev, here, fields = dims
    got, out, other = rest[:chips], rest[-chips - 3 : -3], rest[-3]
    rows, slots = rest[-2:]
    chip, core = me[1], me[2]
    wide = 2 * here
    span = lev_dev * wide
    per = lats * cap
    order = by_column_owner(mine[2:3, : weight.shape[0]], lev_dev, chips, wide)
    for k in range(chips):
        first = pl.multiple_of(xor(chip, k) * span, span)
        for f in range(fields):
            rows[pl.ds(first, span), f * LANES : (f + 1) * LANES] = got[k][f * span : (f + 1) * span]
        other[xor(chip, k)] = got[k][pl.ds(pl.multiple_of(fields * span + (1 - core) * per, 8), per), :]
    for c in range(chips):
        for l in range(lev_dev):
            at = l * chips * wide + c * wide
            rows[c * span + l * wide : c * span + (l + 1) * wide, fields * LANES :] = weight[at : at + wide]
    tables = [slot_table(dims, core, order, False) for core in range(2)]
    res = pick(jnp.concatenate(tables, axis=0), rows[...], (1,))
    for core in range(2):
        for g in range(lats):
            for c in range(chips):
                at = ((core * lats + g) * chips + c) * cap
                for f in range(fields + 1):
                    slots[c, core, g, f] = res[at : at + cap, f * LANES : (f + 1) * LANES]
    for k in range(chips):
        out[k][...] = slots[xor(chip, k)]


def sort_kernel(groups, dims, me, *rest):
    lats, slabs, chips, cap, lev_dev, here, fields = dims
    got, outs = rest[:chips], rest[-len(groups) :]
    lat, chip, core = me[0], me[1], me[2]
    for k in range(chips):
        src = xor(chip, k)
        for out, j in zip(outs, groups):
            for x in range(2):
                for f in range(fields + 1):
                    out[f, x, src] = got[k][x, xor(lat, j), f]


def add_kernel(dims, me, mine, mine_pair, *rest):
    lats, slabs, chips, cap, lev_dev, here, fields = dims
    got, outs, rows = rest[:lats], rest[-3:-1], rest[-1]
    blocks = slabs * here
    row_total = lev_dev * blocks
    slots = lats * chips * cap
    lat, core = me[0], me[2]
    row = iota((row_total, slots), 0)
    for x, (source, out) in enumerate(zip((mine, mine_pair), outs)):
        for j in range(lats):
            for f in range(fields + 1):
                rows[f, xor(lat, j)] = got[j][f, xor(core, x)]
        low = source[pl.ds(core, 1), :slots].astype(jnp.int32)
        scale = jnp.concatenate([rows[fields].reshape(slots, LANES)] * fields, axis=1)
        value = jnp.concatenate([rows[f].reshape(slots, LANES) for f in range(fields)], axis=1)
        values = jnp.concatenate([(1.0 - scale) * value, scale * value], axis=0)
        table = jnp.concatenate([hot(row, low), hot(row, low + blocks)], axis=1)
        total = pick(table, values, (1,))
        for l in range(lev_dev):
            for f in range(fields):
                out[l, f] = total[l * blocks : (l + 1) * blocks, f * LANES : (f + 1) * LANES]


def hold_kernel(dims, me, array, mine, mine_pair, *rest):
    lats, slabs, chips, cap, lev_dev, here, fields = dims
    out, dests, sem = rest[-3:]
    copy = pltpu.make_async_copy(array.at[pl.ds(0, out.shape[0])], out, sem)
    copy.start()
    total = dests.shape[1]
    both = jnp.concatenate([mine[2:3, :total], mine_pair[2:3, :total]], axis=0)
    dests[...] = by_column_owner(both, lev_dev, chips, 2 * here)
    copy.wait()


def mix_kernel(dims, me, weight_pair, *rest):
    lats, slabs, chips, cap, lev_dev, here, fields = dims
    got, packed, at = rest[:chips], [], chips
    for j in range(lats):
        count = 2 if forwarded(j) else 1
        packed.append(rest[at : at + count])
        at += count
    out, weight, mixed = rest[-chips - 2 : -2], rest[-2], rest[-1]
    lat, chip, core = me[0], me[1], me[2]
    blocks = slabs * here
    row_total = lev_dev * blocks
    slots = slabs * cap
    for g in range(lats):
        for k in range(chips):
            at = pl.multiple_of(fields * lev_dev * 2 * here + core * lats * cap, 8) + g * cap
            weight[g, core, xor(chip, k)] = got[k][pl.ds(at, cap), :]
            weight[g, 1 - core, k] = weight_pair[k, g * cap : (g + 1) * cap]
    row = iota((row_total, slots), 0)
    for j in range(lats):
        sender = xor(lat, j)
        tail = fields * row_total - sum(part.shape[0] for part in packed[j][:-1])
        low = packed[j][-1][pl.ds(tail + lat, 1), :][:, :slots].astype(jnp.int32)

        def level_rows(l, f, parts=packed[j]):
            at = (l * fields + f) * blocks
            if at >= parts[0].shape[0]:
                return parts[1][at - parts[0].shape[0] : at - parts[0].shape[0] + blocks]
            return parts[0][at : at + blocks]

        values = jnp.concatenate(
            [
                jnp.concatenate([level_rows(l, f) for l in range(lev_dev)], axis=0)
                for f in range(fields)
            ],
            axis=1,
        )
        table = jnp.concatenate([hot(row, low), hot(row, low + blocks)], axis=1)
        both = pick(table, values, (0,))
        scale = jnp.concatenate([weight[sender].reshape(slots, LANES)] * fields, axis=1)
        res = (1.0 - scale) * both[:slots] + scale * both[slots:]
        for r in range(2):
            for c in range(chips):
                at = (r * chips + c) * cap
                for f in range(fields):
                    mixed[r, c, f] = res[at : at + cap, f * LANES : (f + 1) * LANES]
        for k in range(chips):
            for x in range(2):
                out[k][x, sender] = mixed[xor(core, x), xor(chip, k)]


def arrive_kernel(dims, me, dest, *rest):
    lats, slabs, chips, cap, lev_dev, here, fields = dims
    got, out = rest[:chips], rest[-chips - 2 : -2]
    rows, moved = rest[-2:]
    chip, core = me[1], me[2]
    span = lev_dev * 2 * here
    for x in range(2):
        for k in range(chips):
            for g in range(lats):
                for f in range(fields):
                    rows[f, g * chips + xor(chip, k)] = got[k][x, g, f]
        values = jnp.concatenate(
            [rows[f].reshape(lats * chips * cap, LANES) for f in range(fields)], axis=1
        )
        res = pick(slot_table(dims, core, dest[x : x + 1, :], False), values, (0,))
        for c in range(chips):
            for f in range(fields):
                moved[c, f] = res[c * span : (c + 1) * span, f * LANES : (f + 1) * LANES]
        for k in range(chips):
            for f in range(fields):
                out[k][f, xor(core, x)] = moved[xor(chip, k), f]


def diffuse_kernel(dims, me, inverse, *rest):
    lats, slabs, chips, cap, lev_dev, here, fields = dims
    got, own, pair, rows = rest[:chips], rest[-3], rest[-2], rest[-1]
    chip, core = me[1], me[2]
    wide = 2 * here
    span = 2 * lev_dev * wide
    levels = slabs * lev_dev
    for k in range(chips):
        first = pl.multiple_of(xor(chip, k) * span, span)
        for f in range(fields):
            rows[f, pl.ds(first, span), :] = got[k][f].reshape(span, LANES)
    for f in range(fields):
        values = jnp.concatenate([rows[f, pl.ds(b, levels, stride=wide), :] for b in range(wide)], axis=1)
        res = product(inverse[f], values, (1,))
        first, second = res[:, : here * LANES], res[:, here * LANES :]
        mine, other = jnp.where(core == 0, first, second), jnp.where(core == 0, second, first)
        for b in range(here):
            at = pl.ds(f * here + b, levels, stride=fields * here)
            own[at, :] = mine[:, b * LANES : (b + 1) * LANES]
            pair[at, :] = other[:, b * LANES : (b + 1) * LANES]


def finish_kernel(dims, me, mine, got, *rest):
    out, total, sems = rest[-3:]
    pieces = sems.shape[0]
    step = total.shape[0] // pieces
    copies = []
    for i in range(pieces):
        rows = pl.ds(i * step, step)
        total[rows, :] = mine[rows, :] + got[rows, :]
        copies.append(pltpu.make_async_copy(total.at[rows], out.at[rows], sems.at[i]))
        copies[-1].start()
    for copy in copies:
        copy.wait()


def place():
    slab = lax.axis_index("slab")
    return lax.axis_index("lat"), lax.div(slab, 2), lax.rem(slab, 2)


def call(kernel, dims, args, outs, scratch=(), after=(), outside=False, to_main=False, limit=48):
    inside = pl.BlockSpec(memory_space=pltpu.VMEM)
    anywhere = pl.BlockSpec(memory_space=pl.ANY)
    if outside:
        specs = [anywhere] * len(args)
    else:
        specs = [inside] * len(args)
    return pl.pallas_call(
        functools.partial(kernel, dims) if outside else lambda *refs: kernel(dims, place(), *refs),
        out_shape=[shape if hasattr(shape, "dtype") else jax.ShapeDtypeStruct(shape, F32) for shape in outs],
        in_specs=specs + [anywhere] * len(after),
        out_specs=[anywhere if to_main else inside] * len(outs),
        scratch_shapes=[pltpu.VMEM(shape, F32) if isinstance(shape, tuple) else shape for shape in scratch],
        compiler_params=pltpu.CompilerParams(vmem_limit_bytes=limit * 1024 * 1024),
    )(*args, *after)


def forwarded(j):
    return j % 2 == 1 and j > 1


def swap(array, axis, bit, count):
    return lax.ppermute(array, axis, [(i, i ^ bit) for i in range(count)])


def body(lats, slabs, field_state, cotangent, vertical_weight, diffusion_inverse, source_row, dest_slot):
    _, lev_dev, blocks, fields, width = field_state.shape
    cap = source_row.shape[-1]
    chips = slabs // 2
    here = blocks // slabs
    levels = slabs * lev_dev
    row_total = lev_dev * blocks
    span = lev_dev * 2 * here
    dims = (lats, slabs, chips, cap, lev_dev, here, fields)

    def pair(array):
        return swap(array, "slab", 1, slabs)

    def over_chips(messages):
        got = list(messages)
        for k in reversed(range(1, chips)):
            got[k] = swap(messages[k], "slab", 2 * k, slabs)
        return got

    state = field_state[0].transpose(0, 2, 1, 3).reshape(row_total * fields, width)
    cot = cotangent[0].transpose(0, 2, 1, 3).reshape(levels * fields * here, width)
    weights = vertical_weight.reshape(row_total, width)
    inverse = diffusion_inverse[0]
    dest = dest_slot[0]

    cut = row_total * fields // 2
    packed, second_half, mine, cot_here, weights_here, inverse_here = call(
        pack_kernel,
        dims,
        [
            pltpu.with_memory_space_constraint(array, pltpu.HBM)
            for array in (state, source_row[0, 0], dest, cot, weights, inverse)
        ],
        [
            (row_total * fields + -(-lats // 8) * 8, width),
            (row_total * fields + -(-lats // 8) * 8 - cut, width),
            (8, max(row_total, lats * chips * cap)),
            cot.shape,
            weights.shape,
            inverse.shape,
        ],
        [
            pltpu.VMEM((lats, slabs, cap), jnp.int32),
            pltpu.VMEM(dest.shape, jnp.int32),
            pltpu.SemaphoreType.DMA((7,)),
        ],
        outside=True,
        limit=48,
    )
    mine_pair = pair(mine)
    near, far = swap(packed, "lat", 1, lats), swap(packed, "lat", 2, lats)
    first = over_chips(
        call(
            start_kernel,
            dims,
            (cot_here, inverse_here, pair(cot), weights_here, mine),
            [(fields * span + 2 * lats * cap, width)] * chips,
            [(fields, levels * 2 * here, width), (chips, 2, lats * cap, width)],
        )
    )
    *slot_back, weight_other = call(
        back_kernel,
        dims,
        (mine, weights_here, *first),
        [(2, lats, fields + 1, cap, width)] * chips + [(chips, lats * cap, width)],
        [(row_total, (fields + 1) * width), (chips, 2, lats, fields + 1, cap, width)],
        after=[mine_pair],
    )
    opposite = swap(second_half, "lat", 3, lats)
    first_half, dests = call(
        hold_kernel,
        dims,
        (far, mine, mine_pair),
        [(cut, width), jax.ShapeDtypeStruct((2, row_total), jnp.int32)],
        [pltpu.SemaphoreType.DMA(())],
        after=[slot_back[0], near],
    )
    slot_back = over_chips(slot_back)
    states = []
    for j in range(lats):
        if forwarded(j):
            states.append(swap(first_half if j == 3 else states[-1][:cut], "lat", 1, lats))
            states.append(opposite if j == 3 else swap(second_half, "lat", j, lats))
        else:
            states.append({0: packed, 1: near, 2: far}[j] if j < 3 else swap(packed, "lat", j, lats))
    soon = [j for j in range(lats) if j == 2]
    late = [j for j in range(lats) if j != 2]
    message = (fields + 1, 2, chips, cap, width)
    sorted_soon = call(functools.partial(sort_kernel, soon), dims, slot_back, [message] * len(soon))
    mixed = call(
        mix_kernel,
        dims,
        (pair(weight_other), *first, *states),
        [(2, lats, fields, cap, width)] * chips,
        [(lats, 2, chips, cap, width), (2, chips, fields, cap, width)],
        after=sorted_soon,
    )
    sorted_late = call(
        functools.partial(sort_kernel, late), dims, slot_back, [message] * len(late), after=mixed[:1]
    )
    returned = [None] * lats
    for j, sorted_back in zip(soon + late, [*sorted_soon, *sorted_late]):
        returned[j] = sorted_back if j == 0 else swap(sorted_back, "lat", j, lats)
    moved = call(
        arrive_kernel,
        dims,
        (dests, *over_chips(mixed)),
        [(fields, 2, span, width)] * chips,
        [(fields, lats * chips, cap, width), (chips, fields, span, width)],
        after=returned[2:3],
    )
    moved = over_chips(moved)
    adjoint, adjoint_pair = call(
        add_kernel,
        dims,
        (mine, mine_pair, *returned),
        [(lev_dev, fields, blocks, width)] * 2,
        [(fields + 1, lats, chips, cap, width)],
        after=moved[1:2],
    )
    tangent, tangent_pair = call(
        diffuse_kernel,
        dims,
        (inverse_here, *moved),
        [cot.shape, cot.shape],
        [(fields, levels * 2 * here, width)],
        after=[adjoint_pair],
    )
    adjoint = adjoint + pair(adjoint_pair)
    (tangent,) = call(
        finish_kernel,
        dims,
        (tangent, pair(tangent_pair)),
        [tangent.shape],
        [tangent.shape, pltpu.SemaphoreType.DMA((fields,))],
        after=[adjoint],
        to_main=True,
    )
    tangent_out = tangent.reshape(1, levels, fields, here, width).transpose(0, 1, 3, 2, 4)
    adjoint_out = adjoint.transpose(0, 2, 1, 3)[None]
    return tangent_out, adjoint_out


def solution(mesh):
    placed = (
        P("lat", "slab", None, None, None),
        P("lat", None, "slab", None, None),
        P("lat", "slab", None, None),
        P("lat", None, None, None),
        P("lat", "slab", None, None, None),
        P("lat", "slab", None),
    )
    return jax.shard_map(
        functools.partial(body, mesh.shape["lat"], mesh.shape["slab"]),
        mesh=mesh,
        in_specs=placed,
        out_specs=(P("lat", None, "slab", None, None), P("lat", "slab", None, None, None)),
        check_vma=False,
    )
```

```python
import functools

import jax
import jax.numpy as jnp
from jax import lax
from jax.experimental import pallas as pl
from jax.experimental.pallas import tpu as pltpu
from jax.sharding import PartitionSpec as P

LANES = 128
F32 = jnp.float32
EXACT = functools.partial(lax.dot_general, precision=lax.Precision.HIGHEST, preferred_element_type=F32)
SHORT = functools.partial(lax.dot_general, preferred_element_type=F32)


def two_parts(values):
    high = values.astype(jnp.bfloat16)
    return high, (values - high.astype(F32)).astype(jnp.bfloat16)


def pick(table, values, contract):
    table = jnp.concatenate([table, table], axis=contract[0])
    return SHORT(table, jnp.concatenate(two_parts(values), axis=0), ((contract, (0,)), ((), ())))


def product(left, right, contract):
    left_high, left_low = two_parts(left)
    right_high, right_low = two_parts(right)
    left = jnp.concatenate([left_high, left_low, left_high], axis=contract[0])
    right = jnp.concatenate([right_high, right_high, right_low], axis=0)
    return SHORT(left, right, ((contract, (0,)), ((), ())))


def hot(rows, wanted):
    return jnp.where(rows == wanted, 1.0, 0.0).astype(jnp.bfloat16)


def iota(shape, axis):
    return lax.broadcasted_iota(jnp.int32, shape, axis)


def xor(a, b):
    return jnp.bitwise_xor(a, b)


def pack_kernel(dims, state, source_in, dest_in, cot_in, weight_in, inverse_in, *rest):
    lats, slabs, chips, cap, lev_dev, here, fields = dims
    out, second_half, mine, cot, weight, inverse, source, dest, sems = rest
    total = state.shape[0]
    cut = out.shape[0] - second_half.shape[0]
    copies = [
        pltpu.make_async_copy(src, dst, sems.at[i])
        for i, (src, dst) in enumerate(
            (
                (source_in, source),
                (dest_in, dest),
                (state, out.at[pl.ds(0, total)]),
                (state.at[pl.ds(cut, total - cut)], second_half.at[pl.ds(0, total - cut)]),
                (cot_in, cot),
                (weight_in, weight),
                (inverse_in, inverse),
            )
        )
    ]
    for copy in copies:
        copy.start()
    copies[0].wait()
    copies[1].wait()
    numbers = source[...].reshape(lats * slabs, cap).astype(F32)
    slots = slabs * cap
    row = iota((slabs, slots), 0)
    at = iota((slabs, slots), 1)
    core = at // (chips * cap)
    chosen = row == (at // cap - core * chips) * 2 + core
    spread = jnp.where(iota((cap, slots), 1) % cap == iota((cap, slots), 0), 1.0, 0.0)
    wide = EXACT(numbers, spread, (((1,), (0,)), ((), ())))
    out[total:, :] = jnp.zeros((out.shape[0] - total, LANES), F32)
    for g in range(lats):
        lanes = jnp.where(chosen, wide[g * slabs : (g + 1) * slabs], 0.0)
        out[total + g : total + g + 1, :slots] = jnp.sum(lanes, axis=0, keepdims=True)
    second_half[total - cut :, :] = out[total:, :]
    slots = lats * chips * cap
    row = iota((lats * slabs, slots), 0)
    at = iota((lats * slabs, slots), 1)
    spread = jnp.where(iota((cap, slots), 1) % cap == iota((cap, slots), 0), 1.0, 0.0)
    wide = EXACT(numbers, spread, (((1,), (0,)), ((), ())))
    mine[...] = jnp.zeros(mine.shape, F32)
    for core in range(2):
        lanes = jnp.where(row == at // cap * 2 + core, wide, 0.0)
        mine[core : core + 1, :slots] = jnp.sum(lanes, axis=0, keepdims=True)
    mine[2:3, : dest.shape[1]] = dest[...].astype(F32)
    for copy in copies[2:]:
        copy.wait()


def start_kernel(dims, me, cot, inverse, cot_pair, weight, mine, *rest):
    lats, slabs, chips, cap, lev_dev, here, fields = dims
    out, back, held = rest[:chips], rest[-2], rest[-1]
    chip, core = me[1], me[2]
    levels = slabs * lev_dev
    step = fields * here
    span = lev_dev * 2 * here
    per = lats * cap
    for f in range(fields):
        own = [cot[pl.ds(f * here + b, levels, stride=step), :] for b in range(here)]
        pair = [cot_pair[pl.ds(f * here + b, levels, stride=step), :] for b in range(here)]
        own, pair = jnp.concatenate(own, axis=1), jnp.concatenate(pair, axis=1)
        wide = jnp.concatenate(
            [jnp.where(core == 0, own, pair), jnp.where(core == 0, pair, own)], axis=1
        )
        res = product(inverse[f], wide, (0,))
        for b in range(2 * here):
            back[f, pl.ds(b, levels, stride=2 * here), :] = res[:, b * LANES : (b + 1) * LANES]
    dest = mine[2:3, : weight.shape[0]].astype(jnp.int32)
    for x in range(2):
        res = pick(slot_table(dims, x, dest, True), weight[...], (1,))
        for c in range(chips):
            held[c, x] = res[c * per : (c + 1) * per]
    for k in range(chips):
        to = xor(chip, k)
        first = pl.multiple_of((to * 2 + core) * span, span)
        for f in range(fields):
            out[k][f * span : (f + 1) * span] = back[f, pl.ds(first, span), :]
        for x in range(2):
            at = fields * span + x * per
            out[k][at : at + per] = held[to, x]


def by_column_owner(dest, lev_dev, chips, wide):
    total = dest.shape[1]
    at = iota((total, total), 1)
    span = lev_dev * wide
    chip = at // span
    level = (at - chip * span) // wide
    block = at - chip * span - level * wide
    order = jnp.where(iota((total, total), 0) == (level * chips + chip) * wide + block, 1.0, 0.0)
    return EXACT(dest.astype(F32), order, (((1,), (0,)), ((), ()))).astype(jnp.int32)


def slot_table(dims, core, dest, by_chip):
    lats, slabs, chips, cap, lev_dev, here, fields = dims
    at = iota((lats * chips * cap, dest.shape[1]), 0)
    if by_chip:
        chip = at // (lats * cap)
        lat = at // cap - chip * lats
    else:
        lat = at // (chips * cap)
        chip = at // cap - lat * chips
    slot = at - at // cap * cap
    return hot(lat * (slabs * cap) + (chip * 2 + core) * cap + slot, dest)


def back_kernel(dims, me, mine, weight, *rest):
    lats, slabs, chips, cap, lev_dev, here, fields = dims
    got, out, other = rest[:chips], rest[-chips - 3 : -3], rest[-3]
    rows, slots = rest[-2:]
    chip, core = me[1], me[2]
    wide = 2 * here
    span = lev_dev * wide
    per = lats * cap
    order = by_column_owner(mine[2:3, : weight.shape[0]], lev_dev, chips, wide)
    for k in range(chips):
        first = pl.multiple_of(xor(chip, k) * span, span)
        for f in range(fields):
            rows[pl.ds(first, span), f * LANES : (f + 1) * LANES] = got[k][f * span : (f + 1) * span]
        other[xor(chip, k)] = got[k][pl.ds(pl.multiple_of(fields * span + (1 - core) * per, 8), per), :]
    for c in range(chips):
        for l in range(lev_dev):
            at = l * chips * wide + c * wide
            rows[c * span + l * wide : c * span + (l + 1) * wide, fields * LANES :] = weight[at : at + wide]
    tables = [slot_table(dims, core, order, False) for core in range(2)]
    res = pick(jnp.concatenate(tables, axis=0), rows[...], (1,))
    for core in range(2):
        for g in range(lats):
            for c in range(chips):
                at = ((core * lats + g) * chips + c) * cap
                for f in range(fields + 1):
                    slots[c, core, g, f] = res[at : at + cap, f * LANES : (f + 1) * LANES]
    for k in range(chips):
        out[k][...] = slots[xor(chip, k)]


def sort_kernel(groups, dims, me, *rest):
    lats, slabs, chips, cap, lev_dev, here, fields = dims
    got, outs = rest[:chips], rest[-len(groups) :]
    lat, chip, core = me[0], me[1], me[2]
    for k in range(chips):
        src = xor(chip, k)
        for out, j in zip(outs, groups):
            for x in range(2):
                for f in range(fields + 1):
                    out[f, x, src] = got[k][x, xor(lat, j), f]


def add_kernel(dims, me, mine, mine_pair, *rest):
    lats, slabs, chips, cap, lev_dev, here, fields = dims
    got, outs, rows = rest[:lats], rest[-3:-1], rest[-1]
    blocks = slabs * here
    row_total = lev_dev * blocks
    slots = lats * chips * cap
    lat, core = me[0], me[2]
    row = iota((row_total, slots), 0)
    for x, (source, out) in enumerate(zip((mine, mine_pair), outs)):
        for j in range(lats):
            for f in range(fields + 1):
                rows[f, xor(lat, j)] = got[j][f, xor(core, x)]
        low = source[pl.ds(core, 1), :slots].astype(jnp.int32)
        scale = jnp.concatenate([rows[fields].reshape(slots, LANES)] * fields, axis=1)
        value = jnp.concatenate([rows[f].reshape(slots, LANES) for f in range(fields)], axis=1)
        values = jnp.concatenate([(1.0 - scale) * value, scale * value], axis=0)
        table = jnp.concatenate([hot(row, low), hot(row, low + blocks)], axis=1)
        total = pick(table, values, (1,))
        for l in range(lev_dev):
            for f in range(fields):
                out[l, f] = total[l * blocks : (l + 1) * blocks, f * LANES : (f + 1) * LANES]


def hold_kernel(dims, me, array, mine, mine_pair, *rest):
    lats, slabs, chips, cap, lev_dev, here, fields = dims
    out, dests, sem = rest[-3:]
    copy = pltpu.make_async_copy(array.at[pl.ds(0, out.shape[0])], out, sem)
    copy.start()
    total = dests.shape[1]
    both = jnp.concatenate([mine[2:3, :total], mine_pair[2:3, :total]], axis=0)
    dests[...] = by_column_owner(both, lev_dev, chips, 2 * here)
    copy.wait()


def mix_kernel(dims, me, weight_pair, *rest):
    lats, slabs, chips, cap, lev_dev, here, fields = dims
    got, packed, at = rest[:chips], [], chips
    for j in range(lats):
        count = 2 if forwarded(j) else 1
        packed.append(rest[at : at + count])
        at += count
    out, weight, mixed = rest[-chips - 2 : -2], rest[-2], rest[-1]
    lat, chip, core = me[0], me[1], me[2]
    blocks = slabs * here
    row_total = lev_dev * blocks
    slots = slabs * cap
    for g in range(lats):
        for k in range(chips):
            at = pl.multiple_of(fields * lev_dev * 2 * here + core * lats * cap, 8) + g * cap
            weight[g, core, xor(chip, k)] = got[k][pl.ds(at, cap), :]
            weight[g, 1 - core, k] = weight_pair[k, g * cap : (g + 1) * cap]
    row = iota((row_total, slots), 0)
    for j in range(lats):
        sender = xor(lat, j)
        tail = fields * row_total - sum(part.shape[0] for part in packed[j][:-1])
        low = packed[j][-1][pl.ds(tail + lat, 1), :][:, :slots].astype(jnp.int32)

        def level_rows(l, f, parts=packed[j]):
            at = (l * fields + f) * blocks
            if at >= parts[0].shape[0]:
                return parts[1][at - parts[0].shape[0] : at - parts[0].shape[0] + blocks]
            return parts[0][at : at + blocks]

        values = jnp.concatenate(
            [
                jnp.concatenate([level_rows(l, f) for l in range(lev_dev)], axis=0)
                for f in range(fields)
            ],
            axis=1,
        )
        table = jnp.concatenate([hot(row, low), hot(row, low + blocks)], axis=1)
        both = pick(table, values, (0,))
        scale = jnp.concatenate([weight[sender].reshape(slots, LANES)] * fields, axis=1)
        res = (1.0 - scale) * both[:slots] + scale * both[slots:]
        for r in range(2):
            for c in range(chips):
                at = (r * chips + c) * cap
                for f in range(fields):
                    mixed[r, c, f] = res[at : at + cap, f * LANES : (f + 1) * LANES]
        for k in range(chips):
            for x in range(2):
                out[k][x, sender] = mixed[xor(core, x), xor(chip, k)]


def arrive_kernel(dims, me, dest, *rest):
    lats, slabs, chips, cap, lev_dev, here, fields = dims
    got, out = rest[:chips], rest[-chips - 2 : -2]
    rows, moved = rest[-2:]
    chip, core = me[1], me[2]
    span = lev_dev * 2 * here
    for x in range(2):
        for k in range(chips):
            for g in range(lats):
                for f in range(fields):
                    rows[f, g * chips + xor(chip, k)] = got[k][x, g, f]
        values = jnp.concatenate(
            [rows[f].reshape(lats * chips * cap, LANES) for f in range(fields)], axis=1
        )
        res = pick(slot_table(dims, core, dest[x : x + 1, :], False), values, (0,))
        for c in range(chips):
            for f in range(fields):
                moved[c, f] = res[c * span : (c + 1) * span, f * LANES : (f + 1) * LANES]
        for k in range(chips):
            for f in range(fields):
                out[k][f, xor(core, x)] = moved[xor(chip, k), f]


def diffuse_kernel(dims, me, inverse, *rest):
    lats, slabs, chips, cap, lev_dev, here, fields = dims
    got, own, pair, rows = rest[:chips], rest[-3], rest[-2], rest[-1]
    chip, core = me[1], me[2]
    wide = 2 * here
    span = 2 * lev_dev * wide
    levels = slabs * lev_dev
    for k in range(chips):
        first = pl.multiple_of(xor(chip, k) * span, span)
        for f in range(fields):
            rows[f, pl.ds(first, span), :] = got[k][f].reshape(span, LANES)
    for f in range(fields):
        values = jnp.concatenate([rows[f, pl.ds(b, levels, stride=wide), :] for b in range(wide)], axis=1)
        res = product(inverse[f], values, (1,))
        first, second = res[:, : here * LANES], res[:, here * LANES :]
        mine, other = jnp.where(core == 0, first, second), jnp.where(core == 0, second, first)
        for b in range(here):
            at = pl.ds(f * here + b, levels, stride=fields * here)
            own[at, :] = mine[:, b * LANES : (b + 1) * LANES]
            pair[at, :] = other[:, b * LANES : (b + 1) * LANES]


def finish_kernel(dims, me, mine, got, *rest):
    out, total, sems = rest[-3:]
    pieces = sems.shape[0]
    step = total.shape[0] // pieces
    copies = []
    for i in range(pieces):
        rows = pl.ds(i * step, step)
        total[rows, :] = mine[rows, :] + got[rows, :]
        copies.append(pltpu.make_async_copy(total.at[rows], out.at[rows], sems.at[i]))
        copies[-1].start()
    for copy in copies:
        copy.wait()


def place():
    slab = lax.axis_index("slab")
    return lax.axis_index("lat"), lax.div(slab, 2), lax.rem(slab, 2)


def call(kernel, dims, args, outs, scratch=(), after=(), outside=False, to_main=False, limit=48):
    inside = pl.BlockSpec(memory_space=pltpu.VMEM)
    anywhere = pl.BlockSpec(memory_space=pl.ANY)
    if outside:
        specs = [anywhere] * len(args)
    else:
        specs = [inside] * len(args)
    return pl.pallas_call(
        functools.partial(kernel, dims) if outside else lambda *refs: kernel(dims, place(), *refs),
        out_shape=[shape if hasattr(shape, "dtype") else jax.ShapeDtypeStruct(shape, F32) for shape in outs],
        in_specs=specs + [anywhere] * len(after),
        out_specs=[anywhere if to_main else inside] * len(outs),
        scratch_shapes=[pltpu.VMEM(shape, F32) if isinstance(shape, tuple) else shape for shape in scratch],
        compiler_params=pltpu.CompilerParams(vmem_limit_bytes=limit * 1024 * 1024),
    )(*args, *after)


def forwarded(j):
    return j % 2 == 1 and j > 1


def swap(array, axis, bit, count):
    return lax.ppermute(array, axis, [(i, i ^ bit) for i in range(count)])


def body(lats, slabs, field_state, cotangent, vertical_weight, diffusion_inverse, source_row, dest_slot):
    _, lev_dev, blocks, fields, width = field_state.shape
    cap = source_row.shape[-1]
    chips = slabs // 2
    here = blocks // slabs
    levels = slabs * lev_dev
    row_total = lev_dev * blocks
    span = lev_dev * 2 * here
    dims = (lats, slabs, chips, cap, lev_dev, here, fields)

    def pair(array):
        return swap(array, "slab", 1, slabs)

    def over_chips(messages):
        got = list(messages)
        for k in reversed(range(1, chips)):
            got[k] = swap(messages[k], "slab", 2 * k, slabs)
        return got

    state = field_state[0].transpose(0, 2, 1, 3).reshape(row_total * fields, width)
    cot = cotangent[0].transpose(0, 2, 1, 3).reshape(levels * fields * here, width)
    weights = vertical_weight.reshape(row_total, width)
    inverse = diffusion_inverse[0]
    dest = dest_slot[0]

    cut = blocks * (2 * lev_dev * fields // 5)
    packed, second_half, mine, cot_here, weights_here, inverse_here = call(
        pack_kernel,
        dims,
        [
            pltpu.with_memory_space_constraint(array, pltpu.HBM)
            for array in (state, source_row[0, 0], dest, cot, weights, inverse)
        ],
        [
            (row_total * fields + -(-lats // 8) * 8, width),
            (row_total * fields + -(-lats // 8) * 8 - cut, width),
            (8, max(row_total, lats * chips * cap)),
            cot.shape,
            weights.shape,
            inverse.shape,
        ],
        [
            pltpu.VMEM((lats, slabs, cap), jnp.int32),
            pltpu.VMEM(dest.shape, jnp.int32),
            pltpu.SemaphoreType.DMA((7,)),
        ],
        outside=True,
        limit=48,
    )
    mine_pair = pair(mine)
    near, far = swap(packed, "lat", 1, lats), swap(packed, "lat", 2, lats)
    first = over_chips(
        call(
            start_kernel,
            dims,
            (cot_here, inverse_here, pair(cot), weights_here, mine),
            [(fields * span + 2 * lats * cap, width)] * chips,
            [(fields, levels * 2 * here, width), (chips, 2, lats * cap, width)],
        )
    )
    *slot_back, weight_other = call(
        back_kernel,
        dims,
        (mine, weights_here, *first),
        [(2, lats, fields + 1, cap, width)] * chips + [(chips, lats * cap, width)],
        [(row_total, (fields + 1) * width), (chips, 2, lats, fields + 1, cap, width)],
        after=[mine_pair],
    )
    opposite = swap(second_half, "lat", 3, lats)
    first_half, dests = call(
        hold_kernel,
        dims,
        (far, mine, mine_pair),
        [(cut, width), jax.ShapeDtypeStruct((2, row_total), jnp.int32)],
        [pltpu.SemaphoreType.DMA(())],
        after=[slot_back[0], near],
    )
    slot_back = over_chips(slot_back)
    states = []
    for j in range(lats):
        if forwarded(j):
            states.append(swap(first_half if j == 3 else states[-1][:cut], "lat", 1, lats))
            states.append(opposite if j == 3 else swap(second_half, "lat", j, lats))
        else:
            states.append({0: packed, 1: near, 2: far}[j] if j < 3 else swap(packed, "lat", j, lats))
    soon = [j for j in range(lats) if j == 2]
    late = [j for j in range(lats) if j != 2]
    message = (fields + 1, 2, chips, cap, width)
    sorted_soon = call(functools.partial(sort_kernel, soon), dims, slot_back, [message] * len(soon))
    mixed = call(
        mix_kernel,
        dims,
        (pair(weight_other), *first, *states),
        [(2, lats, fields, cap, width)] * chips,
        [(lats, 2, chips, cap, width), (2, chips, fields, cap, width)],
        after=sorted_soon,
    )
    sorted_late = call(
        functools.partial(sort_kernel, late), dims, slot_back, [message] * len(late), after=mixed[:1]
    )
    returned = [None] * lats
    for j, sorted_back in zip(soon + late, [*sorted_soon, *sorted_late]):
        returned[j] = sorted_back if j == 0 else swap(sorted_back, "lat", j, lats)
    moved = call(
        arrive_kernel,
        dims,
        (dests, *over_chips(mixed)),
        [(fields, 2, span, width)] * chips,
        [(fields, lats * chips, cap, width), (chips, fields, span, width)],
        after=returned[2:3],
    )
    moved = over_chips(moved)
    adjoint, adjoint_pair = call(
        add_kernel,
        dims,
        (mine, mine_pair, *returned),
        [(lev_dev, fields, blocks, width)] * 2,
        [(fields + 1, lats, chips, cap, width)],
        after=moved[1:2],
    )
    tangent, tangent_pair = call(
        diffuse_kernel,
        dims,
        (inverse_here, *moved),
        [cot.shape, cot.shape],
        [(fields, levels * 2 * here, width)],
        after=[adjoint_pair],
    )
    adjoint = adjoint + pair(adjoint_pair)
    (tangent,) = call(
        finish_kernel,
        dims,
        (tangent, pair(tangent_pair)),
        [tangent.shape],
        [tangent.shape, pltpu.SemaphoreType.DMA((fields,))],
        after=[adjoint],
        to_main=True,
    )
    tangent_out = tangent.reshape(1, levels, fields, here, width).transpose(0, 1, 3, 2, 4)
    adjoint_out = adjoint.transpose(0, 2, 1, 3)[None]
    return tangent_out, adjoint_out


def solution(mesh):
    placed = (
        P("lat", "slab", None, None, None),
        P("lat", None, "slab", None, None),
        P("lat", "slab", None, None),
        P("lat", None, None, None),
        P("lat", "slab", None, None, None),
        P("lat", "slab", None),
    )
    return jax.shard_map(
        functools.partial(body, mesh.shape["lat"], mesh.shape["slab"]),
        mesh=mesh,
        in_specs=placed,
        out_specs=(P("lat", None, "slab", None, None), P("lat", "slab", None, None, None)),
        check_vma=False,
    )
```

```python
import functools

import jax
import jax.numpy as jnp
from jax import lax
from jax.experimental import pallas as pl
from jax.experimental.pallas import tpu as pltpu
from jax.sharding import PartitionSpec as P

LANES = 128
F32 = jnp.float32
SHORT = functools.partial(lax.dot_general, preferred_element_type=F32)


def two_parts(values):
    high = values.astype(jnp.bfloat16)
    return high, (values - high.astype(F32)).astype(jnp.bfloat16)


def pick(table, values, contract):
    table = jnp.concatenate([table, table], axis=contract[0])
    return SHORT(table, jnp.concatenate(two_parts(values), axis=0), ((contract, (0,)), ((), ())))


def product(left, right, contract):
    left_high, left_low = two_parts(left)
    right_high, right_low = two_parts(right)
    left = jnp.concatenate([left_high, left_low, left_high], axis=contract[0])
    right = jnp.concatenate([right_high, right_high, right_low], axis=0)
    return SHORT(left, right, ((contract, (0,)), ((), ())))


def place_whole(numbers, table, dims):
    high, low = two_parts(numbers)
    table = table.astype(jnp.bfloat16)
    return SHORT(high, table, dims) + SHORT(low, table, dims)


def hot(rows, wanted):
    return jnp.where(rows == wanted, 1.0, 0.0).astype(jnp.bfloat16)


def iota(shape, axis):
    return lax.broadcasted_iota(jnp.int32, shape, axis)


def xor(a, b):
    return jnp.bitwise_xor(a, b)


def pack_kernel(dims, state, source_in, dest_in, cot_in, weight_in, inverse_in, *rest):
    lats, slabs, chips, cap, lev_dev, here, fields = dims
    out, second_half, mine, cot, weight, inverse, source, dest, sems = rest
    total = state.shape[0]
    cut = out.shape[0] - second_half.shape[0]
    copies = [
        pltpu.make_async_copy(src, dst, sems.at[i])
        for i, (src, dst) in enumerate(
            (
                (source_in, source),
                (dest_in, dest),
                (state, out.at[pl.ds(0, total)]),
                (state.at[pl.ds(cut, total - cut)], second_half.at[pl.ds(0, total - cut)]),
                (cot_in, cot),
                (weight_in, weight),
                (inverse_in, inverse),
            )
        )
    ]
    for copy in copies:
        copy.start()
    copies[0].wait()
    copies[1].wait()
    numbers = source[...].reshape(lats * slabs, cap).astype(F32)
    slots = slabs * cap
    row = iota((slabs, slots), 0)
    at = iota((slabs, slots), 1)
    core = at // (chips * cap)
    chosen = row == (at // cap - core * chips) * 2 + core
    spread = jnp.where(iota((cap, slots), 1) % cap == iota((cap, slots), 0), 1.0, 0.0)
    wide = place_whole(numbers, spread, (((1,), (0,)), ((), ())))
    out[total:, :] = jnp.zeros((out.shape[0] - total, LANES), F32)
    for g in range(lats):
        lanes = jnp.where(chosen, wide[g * slabs : (g + 1) * slabs], 0.0)
        out[total + g : total + g + 1, :slots] = jnp.sum(lanes, axis=0, keepdims=True)
    second_half[total - cut :, :] = out[total:, :]
    slots = lats * chips * cap
    row = iota((lats * slabs, slots), 0)
    at = iota((lats * slabs, slots), 1)
    spread = jnp.where(iota((cap, slots), 1) % cap == iota((cap, slots), 0), 1.0, 0.0)
    wide = place_whole(numbers, spread, (((1,), (0,)), ((), ())))
    mine[...] = jnp.zeros(mine.shape, F32)
    for core in range(2):
        lanes = jnp.where(row == at // cap * 2 + core, wide, 0.0)
        mine[core : core + 1, :slots] = jnp.sum(lanes, axis=0, keepdims=True)
    mine[2:3, : dest.shape[1]] = dest[...].astype(F32)
    for copy in copies[2:]:
        copy.wait()


def start_kernel(dims, me, cot, inverse, cot_pair, weight, mine, *rest):
    lats, slabs, chips, cap, lev_dev, here, fields = dims
    out, back, held = rest[:chips], rest[-2], rest[-1]
    chip, core = me[1], me[2]
    levels = slabs * lev_dev
    step = fields * here
    span = lev_dev * 2 * here
    per = lats * cap
    for f in range(fields):
        own = [cot[pl.ds(f * here + b, levels, stride=step), :] for b in range(here)]
        pair = [cot_pair[pl.ds(f * here + b, levels, stride=step), :] for b in range(here)]
        own, pair = jnp.concatenate(own, axis=1), jnp.concatenate(pair, axis=1)
        wide = jnp.concatenate(
            [jnp.where(core == 0, own, pair), jnp.where(core == 0, pair, own)], axis=1
        )
        res = product(inverse[f], wide, (0,))
        for b in range(2 * here):
            back[f, pl.ds(b, levels, stride=2 * here), :] = res[:, b * LANES : (b + 1) * LANES]
    dest = mine[2:3, : weight.shape[0]].astype(jnp.int32)
    for x in range(2):
        res = pick(slot_table(dims, x, dest, True), weight[...], (1,))
        for c in range(chips):
            held[c, x] = res[c * per : (c + 1) * per]
    for k in range(chips):
        to = xor(chip, k)
        first = pl.multiple_of((to * 2 + core) * span, span)
        for f in range(fields):
            out[k][f * span : (f + 1) * span] = back[f, pl.ds(first, span), :]
        for x in range(2):
            at = fields * span + x * per
            out[k][at : at + per] = held[to, x]


def by_column_owner(dest, lev_dev, chips, wide):
    total = dest.shape[1]
    at = iota((total, total), 1)
    span = lev_dev * wide
    chip = at // span
    level = (at - chip * span) // wide
    block = at - chip * span - level * wide
    order = jnp.where(iota((total, total), 0) == (level * chips + chip) * wide + block, 1.0, 0.0)
    return place_whole(dest.astype(F32), order, (((1,), (0,)), ((), ()))).astype(jnp.int32)


def slot_table(dims, core, dest, by_chip):
    lats, slabs, chips, cap, lev_dev, here, fields = dims
    at = iota((lats * chips * cap, dest.shape[1]), 0)
    if by_chip:
        chip = at // (lats * cap)
        lat = at // cap - chip * lats
    else:
        lat = at // (chips * cap)
        chip = at // cap - lat * chips
    slot = at - at // cap * cap
    return hot(lat * (slabs * cap) + (chip * 2 + core) * cap + slot, dest)


def back_kernel(dims, me, mine, weight, *rest):
    lats, slabs, chips, cap, lev_dev, here, fields = dims
    got, out, other = rest[:chips], rest[-chips - 3 : -3], rest[-3]
    rows, slots = rest[-2:]
    chip, core = me[1], me[2]
    wide = 2 * here
    span = lev_dev * wide
    per = lats * cap
    order = by_column_owner(mine[2:3, : weight.shape[0]], lev_dev, chips, wide)
    for k in range(chips):
        first = pl.multiple_of(xor(chip, k) * span, span)
        for f in range(fields):
            rows[pl.ds(first, span), f * LANES : (f + 1) * LANES] = got[k][f * span : (f + 1) * span]
        other[xor(chip, k)] = got[k][pl.ds(pl.multiple_of(fields * span + (1 - core) * per, 8), per), :]
    for c in range(chips):
        for l in range(lev_dev):
            at = l * chips * wide + c * wide
            rows[c * span + l * wide : c * span + (l + 1) * wide, fields * LANES :] = weight[at : at + wide]
    tables = [slot_table(dims, core, order, False) for core in range(2)]
    res = pick(jnp.concatenate(tables, axis=0), rows[...], (1,))
    for core in range(2):
        for g in range(lats):
            for c in range(chips):
                at = ((core * lats + g) * chips + c) * cap
                for f in range(fields + 1):
                    slots[c, core, g, f] = res[at : at + cap, f * LANES : (f + 1) * LANES]
    for k in range(chips):
        out[k][...] = slots[xor(chip, k)]


def sort_kernel(groups, dims, me, *rest):
    lats, slabs, chips, cap, lev_dev, here, fields = dims
    got, outs = rest[:chips], rest[-len(groups) :]
    lat, chip, core = me[0], me[1], me[2]
    for k in range(chips):
        src = xor(chip, k)
        for out, j in zip(outs, groups):
            for x in range(2):
                for f in range(fields + 1):
                    out[f, x, src] = got[k][x, xor(lat, j), f]


def add_kernel(dims, me, mine, mine_pair, *rest):
    lats, slabs, chips, cap, lev_dev, here, fields = dims
    got, outs, rows = rest[:lats], rest[-3:-1], rest[-1]
    blocks = slabs * here
    row_total = lev_dev * blocks
    slots = lats * chips * cap
    lat, core = me[0], me[2]
    row = iota((row_total, slots), 0)
    for x, (source, out) in enumerate(zip((mine, mine_pair), outs)):
        for j in range(lats):
            for f in range(fields + 1):
                rows[f, xor(lat, j)] = got[j][f, xor(core, x)]
        low = source[pl.ds(core, 1), :slots].astype(jnp.int32)
        scale = jnp.concatenate([rows[fields].reshape(slots, LANES)] * fields, axis=1)
        value = jnp.concatenate([rows[f].reshape(slots, LANES) for f in range(fields)], axis=1)
        values = jnp.concatenate([(1.0 - scale) * value, scale * value], axis=0)
        table = jnp.concatenate([hot(row, low), hot(row, low + blocks)], axis=1)
        total = pick(table, values, (1,))
        for l in range(lev_dev):
            for f in range(fields):
                out[l, f] = total[l * blocks : (l + 1) * blocks, f * LANES : (f + 1) * LANES]


def hold_kernel(dims, me, array, mine, mine_pair, *rest):
    lats, slabs, chips, cap, lev_dev, here, fields = dims
    out, dests, sem = rest[-3:]
    copy = pltpu.make_async_copy(array.at[pl.ds(0, out.shape[0])], out, sem)
    copy.start()
    total = dests.shape[1]
    both = jnp.concatenate([mine[2:3, :total], mine_pair[2:3, :total]], axis=0)
    dests[...] = by_column_owner(both, lev_dev, chips, 2 * here)
    copy.wait()


def mix_kernel(dims, me, weight_pair, *rest):
    lats, slabs, chips, cap, lev_dev, here, fields = dims
    got, packed, at = rest[:chips], [], chips
    for j in range(lats):
        count = 2 if forwarded(j) else 1
        packed.append(rest[at : at + count])
        at += count
    out, weight, mixed = rest[-chips - 2 : -2], rest[-2], rest[-1]
    lat, chip, core = me[0], me[1], me[2]
    blocks = slabs * here
    row_total = lev_dev * blocks
    slots = slabs * cap
    for g in range(lats):
        for k in range(chips):
            at = pl.multiple_of(fields * lev_dev * 2 * here + core * lats * cap, 8) + g * cap
            weight[g, core, xor(chip, k)] = got[k][pl.ds(at, cap), :]
            weight[g, 1 - core, k] = weight_pair[k, g * cap : (g + 1) * cap]
    row = iota((row_total, slots), 0)
    for j in range(lats):
        sender = xor(lat, j)
        tail = fields * row_total - sum(part.shape[0] for part in packed[j][:-1])
        low = packed[j][-1][pl.ds(tail + lat, 1), :][:, :slots].astype(jnp.int32)

        def level_rows(l, f, parts=packed[j]):
            at = (l * fields + f) * blocks
            if at >= parts[0].shape[0]:
                return parts[1][at - parts[0].shape[0] : at - parts[0].shape[0] + blocks]
            return parts[0][at : at + blocks]

        values = jnp.concatenate(
            [
                jnp.concatenate([level_rows(l, f) for l in range(lev_dev)], axis=0)
                for f in range(fields)
            ],
            axis=1,
        )
        table = jnp.concatenate([hot(row, low), hot(row, low + blocks)], axis=1)
        both = pick(table, values, (0,))
        scale = jnp.concatenate([weight[sender].reshape(slots, LANES)] * fields, axis=1)
        res = (1.0 - scale) * both[:slots] + scale * both[slots:]
        for r in range(2):
            for c in range(chips):
                at = (r * chips + c) * cap
                for f in range(fields):
                    mixed[r, c, f] = res[at : at + cap, f * LANES : (f + 1) * LANES]
        for k in range(chips):
            for x in range(2):
                out[k][x, sender] = mixed[xor(core, x), xor(chip, k)]


def arrive_kernel(dims, me, dest, *rest):
    lats, slabs, chips, cap, lev_dev, here, fields = dims
    got, out = rest[:chips], rest[-chips - 2 : -2]
    rows, moved = rest[-2:]
    chip, core = me[1], me[2]
    span = lev_dev * 2 * here
    for x in range(2):
        for k in range(chips):
            for g in range(lats):
                for f in range(fields):
                    rows[f, g * chips + xor(chip, k)] = got[k][x, g, f]
        values = jnp.concatenate(
            [rows[f].reshape(lats * chips * cap, LANES) for f in range(fields)], axis=1
        )
        res = pick(slot_table(dims, core, dest[x : x + 1, :], False), values, (0,))
        for c in range(chips):
            for f in range(fields):
                moved[c, f] = res[c * span : (c + 1) * span, f * LANES : (f + 1) * LANES]
        for k in range(chips):
            for f in range(fields):
                out[k][f, xor(core, x)] = moved[xor(chip, k), f]


def diffuse_kernel(dims, me, inverse, *rest):
    lats, slabs, chips, cap, lev_dev, here, fields = dims
    got, own, pair, rows = rest[:chips], rest[-3], rest[-2], rest[-1]
    chip, core = me[1], me[2]
    wide = 2 * here
    span = 2 * lev_dev * wide
    levels = slabs * lev_dev
    for k in range(chips):
        first = pl.multiple_of(xor(chip, k) * span, span)
        for f in range(fields):
            rows[f, pl.ds(first, span), :] = got[k][f].reshape(span, LANES)
    for f in range(fields):
        values = jnp.concatenate([rows[f, pl.ds(b, levels, stride=wide), :] for b in range(wide)], axis=1)
        res = product(inverse[f], values, (1,))
        first, second = res[:, : here * LANES], res[:, here * LANES :]
        mine, other = jnp.where(core == 0, first, second), jnp.where(core == 0, second, first)
        for b in range(here):
            at = pl.ds(f * here + b, levels, stride=fields * here)
            own[at, :] = mine[:, b * LANES : (b + 1) * LANES]
            pair[at, :] = other[:, b * LANES : (b + 1) * LANES]


def finish_kernel(dims, me, mine, got, *rest):
    out, total, sems = rest[-3:]
    pieces = sems.shape[0]
    step = total.shape[0] // pieces
    copies = []
    for i in range(pieces):
        rows = pl.ds(i * step, step)
        total[rows, :] = mine[rows, :] + got[rows, :]
        copies.append(pltpu.make_async_copy(total.at[rows], out.at[rows], sems.at[i]))
        copies[-1].start()
    for copy in copies:
        copy.wait()


def place():
    slab = lax.axis_index("slab")
    return lax.axis_index("lat"), lax.div(slab, 2), lax.rem(slab, 2)


def call(kernel, dims, args, outs, scratch=(), after=(), outside=False, to_main=False, limit=48):
    inside = pl.BlockSpec(memory_space=pltpu.VMEM)
    anywhere = pl.BlockSpec(memory_space=pl.ANY)
    if outside:
        specs = [anywhere] * len(args)
    else:
        specs = [inside] * len(args)
    return pl.pallas_call(
        functools.partial(kernel, dims) if outside else lambda *refs: kernel(dims, place(), *refs),
        out_shape=[shape if hasattr(shape, "dtype") else jax.ShapeDtypeStruct(shape, F32) for shape in outs],
        in_specs=specs + [anywhere] * len(after),
        out_specs=[anywhere if to_main else inside] * len(outs),
        scratch_shapes=[pltpu.VMEM(shape, F32) if isinstance(shape, tuple) else shape for shape in scratch],
        compiler_params=pltpu.CompilerParams(vmem_limit_bytes=limit * 1024 * 1024),
    )(*args, *after)


def forwarded(j):
    return j % 2 == 1 and j > 1


def swap(array, axis, bit, count):
    return lax.ppermute(array, axis, [(i, i ^ bit) for i in range(count)])


def body(lats, slabs, field_state, cotangent, vertical_weight, diffusion_inverse, source_row, dest_slot):
    _, lev_dev, blocks, fields, width = field_state.shape
    cap = source_row.shape[-1]
    chips = slabs // 2
    here = blocks // slabs
    levels = slabs * lev_dev
    row_total = lev_dev * blocks
    span = lev_dev * 2 * here
    dims = (lats, slabs, chips, cap, lev_dev, here, fields)

    def pair(array):
        return swap(array, "slab", 1, slabs)

    def over_chips(messages):
        got = list(messages)
        for k in reversed(range(1, chips)):
            got[k] = swap(messages[k], "slab", 2 * k, slabs)
        return got

    state = field_state[0].transpose(0, 2, 1, 3).reshape(row_total * fields, width)
    cot = cotangent[0].transpose(0, 2, 1, 3).reshape(levels * fields * here, width)
    weights = vertical_weight.reshape(row_total, width)
    inverse = diffusion_inverse[0]
    dest = dest_slot[0]

    cut = blocks * (2 * lev_dev * fields // 5)
    packed, second_half, mine, cot_here, weights_here, inverse_here = call(
        pack_kernel,
        dims,
        [
            pltpu.with_memory_space_constraint(array, pltpu.HBM)
            for array in (state, source_row[0, 0], dest, cot, weights, inverse)
        ],
        [
            (row_total * fields + -(-lats // 8) * 8, width),
            (row_total * fields + -(-lats // 8) * 8 - cut, width),
            (8, max(row_total, lats * chips * cap)),
            cot.shape,
            weights.shape,
            inverse.shape,
        ],
        [
            pltpu.VMEM((lats, slabs, cap), jnp.int32),
            pltpu.VMEM(dest.shape, jnp.int32),
            pltpu.SemaphoreType.DMA((7,)),
        ],
        outside=True,
        limit=48,
    )
    mine_pair = pair(mine)
    near, far = swap(packed, "lat", 1, lats), swap(packed, "lat", 2, lats)
    first = over_chips(
        call(
            start_kernel,
            dims,
            (cot_here, inverse_here, pair(cot), weights_here, mine),
            [(fields * span + 2 * lats * cap, width)] * chips,
            [(fields, levels * 2 * here, width), (chips, 2, lats * cap, width)],
        )
    )
    *slot_back, weight_other = call(
        back_kernel,
        dims,
        (mine, weights_here, *first),
        [(2, lats, fields + 1, cap, width)] * chips + [(chips, lats * cap, width)],
        [(row_total, (fields + 1) * width), (chips, 2, lats, fields + 1, cap, width)],
        after=[mine_pair],
    )
    opposite = swap(second_half, "lat", 3, lats)
    first_half, dests = call(
        hold_kernel,
        dims,
        (far, mine, mine_pair),
        [(cut, width), jax.ShapeDtypeStruct((2, row_total), jnp.int32)],
        [pltpu.SemaphoreType.DMA(())],
        after=[slot_back[0], near],
    )
    slot_back = over_chips(slot_back)
    states = []
    for j in range(lats):
        if forwarded(j):
            states.append(swap(first_half if j == 3 else states[-1][:cut], "lat", 1, lats))
            states.append(opposite if j == 3 else swap(second_half, "lat", j, lats))
        else:
            states.append({0: packed, 1: near, 2: far}[j] if j < 3 else swap(packed, "lat", j, lats))
    soon = [j for j in range(lats) if j == 2]
    late = [j for j in range(lats) if j != 2]
    message = (fields + 1, 2, chips, cap, width)
    sorted_soon = call(functools.partial(sort_kernel, soon), dims, slot_back, [message] * len(soon))
    mixed = call(
        mix_kernel,
        dims,
        (pair(weight_other), *first, *states),
        [(2, lats, fields, cap, width)] * chips,
        [(lats, 2, chips, cap, width), (2, chips, fields, cap, width)],
        after=sorted_soon,
    )
    sorted_late = call(
        functools.partial(sort_kernel, late), dims, slot_back, [message] * len(late), after=mixed[:1]
    )
    returned = [None] * lats
    for j, sorted_back in zip(soon + late, [*sorted_soon, *sorted_late]):
        returned[j] = sorted_back if j == 0 else swap(sorted_back, "lat", j, lats)
    moved = call(
        arrive_kernel,
        dims,
        (dests, *over_chips(mixed)),
        [(fields, 2, span, width)] * chips,
        [(fields, lats * chips, cap, width), (chips, fields, span, width)],
        after=returned[2:3],
    )
    moved = over_chips(moved)
    adjoint, adjoint_pair = call(
        add_kernel,
        dims,
        (mine, mine_pair, *returned),
        [(lev_dev, fields, blocks, width)] * 2,
        [(fields + 1, lats, chips, cap, width)],
        after=moved[1:2],
    )
    tangent, tangent_pair = call(
        diffuse_kernel,
        dims,
        (inverse_here, *moved),
        [cot.shape, cot.shape],
        [(fields, levels * 2 * here, width)],
        after=[adjoint_pair],
    )
    adjoint = adjoint + pair(adjoint_pair)
    (tangent,) = call(
        finish_kernel,
        dims,
        (tangent, pair(tangent_pair)),
        [tangent.shape],
        [tangent.shape, pltpu.SemaphoreType.DMA((fields,))],
        after=[adjoint],
        to_main=True,
    )
    tangent_out = tangent.reshape(1, levels, fields, here, width).transpose(0, 1, 3, 2, 4)
    adjoint_out = adjoint.transpose(0, 2, 1, 3)[None]
    return tangent_out, adjoint_out


def solution(mesh):
    placed = (
        P("lat", "slab", None, None, None),
        P("lat", None, "slab", None, None),
        P("lat", "slab", None, None),
        P("lat", None, None, None),
        P("lat", "slab", None, None, None),
        P("lat", "slab", None),
    )
    return jax.shard_map(
        functools.partial(body, mesh.shape["lat"], mesh.shape["slab"]),
        mesh=mesh,
        in_specs=placed,
        out_specs=(P("lat", None, "slab", None, None), P("lat", "slab", None, None, None)),
        check_vma=False,
    )
```
